32 devices in a mesh: member: 4 (over z), dp: 8 (over y, x, core).
Axes of the slice: x: 2, y: 2, z: 4, core: 2. Of those that a mesh axis runs over, the one named last changes fastest.
Arguments:
- teacher_feats: bfloat16 [4, 128, 1024], P('member', 'dp'), may hold values from -8 to 8
- teacher_gain: float32 [4, 1024], P('member'), may hold values from 0.1 to 1.9
- teacher_head: bfloat16 [4, 1024, 3072], P('member', None, 'dp'), may hold values from -1 to 1
- teacher_bias: float32 [4, 3072], P('member', 'dp'), may hold values from -1 to 4
- student_feats: bfloat16 [128, 1024], P('member'), may hold values from -6 to 6
- student_gain: float32 [1024], replicated, may hold values from 0.1 to 1.9
- student_head: bfloat16 [1024, 3072], P('member', 'dp'), may hold values from -0.1875 to 0.1875
- student_bias: float32 [3072], P('dp'), may hold values from -1 to 4
Outputs:
- loss: float32 [], replicated
- head_grad: float32 [1024, 3072], P('member', 'dp')
- bias_grad: float32 [3072], P('dp')
The draws below stay inside these ranges and needn't reach their ends.
All inputs are finite; a program needn't handle non-finite values.
Results may differ from the reference program's by a relative error of at most 0.022.
Values may be sent and summed in bfloat16 or wider, within the bound.
No kernel may reach another device: no remote copies, remote signals or barrier semaphores. Data moves between devices by JAX's collectives and lax.ppermute only.
A program may use at most 64 MiB of HBM per device.

```python
import math
import jax
import jax.numpy as jnp
from jax import lax

D = 1024
MEMBERS = 4
IMAGES = 128
CLASSES = 3072


def teacher_pair(key):
    base_key = jax.random.fold_in(key, 7101)
    subkeys = jax.random.split(base_key, 2)
    features = jax.random.normal(subkeys[0], (MEMBERS, IMAGES, D), jnp.float32)
    weights = jnp.clip(jax.random.normal(subkeys[1], (MEMBERS, D, CLASSES), jnp.float32), -5.0, 5.0) * (3.0 / math.sqrt(D))
    features = jnp.clip(features, -6.0, 6.0)
    return (features, weights)


def rising_offsets(key, salt, shape):
    sub_key = jax.random.fold_in(key, salt)
    position = lax.broadcasted_iota(jnp.float32, shape, len(shape) - 1) / CLASSES
    return jax.random.uniform(sub_key, shape, jnp.float32, -1.0, 1.0) + 1.1 * position


def draw_teacher_feats(key, part):
    return teacher_pair(key)[0].astype(jnp.bfloat16)


def draw_teacher_head(key, part):
    return teacher_pair(key)[1].astype(jnp.bfloat16)


def draw_teacher_bias(key, part):
    return rising_offsets(key, 7202, (MEMBERS, CLASSES))


def draw_student_bias(key, part):
    return rising_offsets(key, 7303, (CLASSES,))


def strengthened(entries, rng, source, target, parts, factor):
    owner, partner = [(jnp.arange(entries.shape[dim]) // (entries.shape[dim] // parts)).reshape([-1 if axis == dim else 1 for axis in range(entries.ndim)]) for dim in (source, target)]
    chosen = jax.random.permutation(rng, parts)[partner]
    strong = (owner == chosen) | (owner == (partner + parts // 2) % parts)
    return jnp.where(strong, factor * entries, entries)


def level_of(rng, extent, shards, smallest, largest):
    def one(dim, parts):
        draws = jax.random.uniform(jax.random.fold_in(jax.random.fold_in(rng, 6), dim), (parts,), jnp.float32, smallest / len(shards), largest / len(shards))
        return jnp.repeat(jnp.exp(draws), extent[dim] // parts).reshape((-1,) + (1,) * (len(extent) - dim - 1))

    level = one(*shards[0])
    for cut in shards[1:]:
        level = level * one(*cut)
    return level


def scatter_about(own_key, shape, width, bound, shards=(), held_as=jnp.bfloat16):
    entries = width * jax.random.normal(own_key, shape, jnp.float32)
    if shards:
        entries = entries * level_of(own_key, shape, shards, -0.22, 0.18)
    return jnp.clip(entries, -bound, bound).astype(held_as)


def heavy_noise(rng, extent, scale, reach, cuts, heavy, dtype=jnp.bfloat16):
    result = scale * jax.random.normal(rng, extent, jnp.float32)
    if cuts:
        result = result * level_of(rng, extent, cuts, -0.22, 0.18)
    return jnp.clip(strengthened(result, jax.random.fold_in(rng, 3), *heavy), -reach, reach).astype(dtype)


def setup_inputs(seed: int = 0) -> dict:
    splits = jax.random.split(jax.random.key(seed), 9)
    teacher_feats = draw_teacher_feats(jax.random.fold_in(splits[8], 71), 0)
    teacher_gain = jnp.clip(1.0 + 0.18 * jax.random.normal(splits[1], (MEMBERS, D), jnp.float32), 0.1, 1.9)
    teacher_head = draw_teacher_head(jax.random.fold_in(splits[8], 71), 0)
    teacher_bias = draw_teacher_bias(jax.random.fold_in(splits[8], 71), 0)
    student_feats = heavy_noise(splits[4], (IMAGES, D), 1.0, 6.0, ((0, 4),), (0, 1, 4, 2.0))
    student_gain = jnp.clip(1.0 + 0.18 * jax.random.normal(splits[5], (D,), jnp.float32), 0.1, 1.9)
    student_head = scatter_about(splits[6], (D, CLASSES), D ** -0.5, 0.1875, ((0, 4), (1, 8)))
    student_bias = draw_student_bias(jax.random.fold_in(splits[8], 71), 0)
    return dict(teacher_feats=teacher_feats, teacher_gain=teacher_gain, teacher_head=teacher_head, teacher_bias=teacher_bias, student_feats=student_feats, student_gain=student_gain, student_head=student_head, student_bias=student_bias)


def norm_rows(values, gain_row):
    values = values.astype(jnp.float32)
    center = values - lax.optimization_barrier(jnp.mean(values, axis=-1, keepdims=True))
    spread = lax.optimization_barrier(jnp.mean(center * center, axis=-1, keepdims=True))
    return center * lax.rsqrt(spread + 1e-06) * gain_row

def reference(teacher_feats, teacher_gain, teacher_head, teacher_bias, student_feats, student_gain, student_head, student_bias):
    members = teacher_feats.shape[0]
    images = teacher_feats.shape[1]

    def member_step(running, inputs):
        features, gain_row, weights, offsets = inputs
        normed = norm_rows(features, gain_row).astype(jnp.bfloat16)
        logits = jnp.dot(normed, weights, preferred_element_type=jnp.float32) + offsets
        maxima = lax.optimization_barrier(jnp.max(logits, axis=1, keepdims=True))
        log_norm = maxima + jnp.log(lax.optimization_barrier(jnp.sum(jnp.exp(logits - maxima), axis=1, keepdims=True)))
        rounded = lax.optimization_barrier((logits - log_norm).astype(jnp.bfloat16))
        return (running + rounded.astype(jnp.float32), None)
    summed, _ = lax.scan(member_step, jnp.zeros((images, CLASSES), jnp.float32), (teacher_feats, teacher_gain, teacher_head, teacher_bias))
    target = summed / members
    normed_s = norm_rows(student_feats, student_gain).astype(jnp.bfloat16)
    alphas = jnp.exp(jnp.dot(normed_s, student_head, preferred_element_type=jnp.float32) + student_bias)
    alpha_sum = lax.optimization_barrier(jnp.sum(alphas, axis=1, keepdims=True))
    per_image = -lax.lgamma(alpha_sum[:, 0]) + lax.optimization_barrier(jnp.sum(lax.lgamma(alphas) - (alphas - 1.0) * target, axis=1))
    loss_value = jnp.sum(per_image) / (images * CLASSES)
    signal = alphas * (lax.digamma(alphas) - lax.digamma(alpha_sum) - target)
    head_grad = lax.dot_general(normed_s.astype(jnp.float32), signal, (((0,), (0,)), ((), ())), precision=lax.Precision.HIGHEST, preferred_element_type=jnp.float32) / images
    bias_grad = lax.optimization_barrier(jnp.sum(signal, axis=0)) / images
    return (loss_value, head_grad, bias_grad)
```

```python
import functools
import math

import jax
import jax.numpy as jnp
from jax import lax
from jax.experimental import pallas as pl
from jax.experimental.pallas import tpu as pltpu
from jax.sharding import PartitionSpec as P

BF16, F32 = jnp.bfloat16, jnp.float32
LANES = 128
PAD = 16
LANCZOS = (
    0.99999999999980993227684700473478,
    676.520368121885098567009190444019,
    -1259.13921672240287047156078755283,
    771.3234287776530788486528258894,
    -176.61502916214059906584551354,
    12.507343278686904814458936853,
    -0.13857109526572011689554707,
    9.984369578019570859563e-6,
    1.50563273514931155834e-7,
)


def partner(index, k, size):
    return index ^ k if size & (size - 1) == 0 else (index + k) % size


def sender(index, k, size):
    return index ^ k if size & (size - 1) == 0 else (index - k + size) % size


def mixed(index, k, size, of):
    if size & (size - 1) == 0:
        return lax.bitwise_xor(index, jnp.int32(k))
    step = k if of is partner else size - k
    return lax.rem(index + jnp.int32(step), jnp.int32(size))


def send(value, axis, k, scale=1, groups=1):
    size = lax.axis_size(axis) // scale
    pairs = [
        (outer * scale + inner, partner(outer, k, size) * scale + inner)
        for outer in range(size)
        for inner in range(scale)
    ]
    return lax.ppermute(value, axis, pairs)


def swap_cores(value, axis):
    return lax.ppermute(value, axis, [(i, i ^ 1) for i in range(lax.axis_size(axis))])


def normed(values, gain_row):
    values = values.astype(F32)
    center = values - jnp.mean(values, axis=-1, keepdims=True)
    spread = jnp.mean(center * center, axis=-1, keepdims=True)
    return (center * lax.rsqrt(spread + 1e-06) * gain_row).astype(BF16)


def split3(value):
    high = value.astype(BF16)
    rest = value - high.astype(F32)
    middle = rest.astype(BF16)
    return high, middle, (rest - middle.astype(F32)).astype(BF16)


def diagonal(rows, lanes):
    return lax.broadcasted_iota(jnp.int32, (rows, lanes), 0) == lax.broadcasted_iota(
        jnp.int32, (rows, lanes), 1
    )


def to_lanes(column, lanes):
    return jnp.sum(
        jnp.where(diagonal(column.shape[0], lanes), column, 0.0), axis=0, keepdims=True
    )


def to_column(row, rows):
    return jnp.sum(jnp.where(diagonal(rows, row.shape[1]), row, 0.0), axis=1, keepdims=True)


def series(x):
    total = jnp.full_like(x, LANCZOS[0])
    slope = jnp.zeros_like(x)
    for k in range(1, 9):
        inverse = 1.0 / (x + float(k))
        term = LANCZOS[k] * inverse
        total = total + term
        slope = slope - term * inverse
    log_t = math.log(7.5) + jnp.log1p(x / 7.5)
    return total, slope, log_t


def log_gamma(x, log_x):
    total, _, log_t = series(x)
    t = x + 7.5
    return (
        (x + 0.5 - t / log_t) * log_t
        + 0.5 * math.log(2.0 * math.pi)
        + jnp.log(total)
        - log_x
    )


def di_gamma(x):
    total, slope, log_t = series(x)
    return log_t + slope / total - 7.0 / (x + 7.5) - 1.0 / x


def student_rows(members, feats_ref, gain_ref, *refs):
    outs, held = refs[:members], refs[members]
    mine = lax.axis_index("member")
    held[...] = normed(feats_ref[...], gain_ref[...])
    width = outs[0].shape[1]
    for k in range(members):
        at = mixed(mine, k, members, partner)
        if width % LANES == 0:
            outs[k][...] = held[:, pl.ds(pl.multiple_of(at * width, LANES), width)]
            continue
        for j in range(members):

            @pl.when(at == j)
            def _(k=k, j=j):
                outs[k][...] = held[:, j * width : (j + 1) * width]


def logits_kernel(members, peers, *refs):
    feats, refs = refs[:peers], refs[peers:]
    gain_ref, head_ref, bias_ref, refs = refs[0], refs[1], refs[2], refs[3:]
    columns, refs = refs[:members], refs[members:]
    student_ref, refs = refs[0], refs[1:]
    payloads, refs = refs[:members], refs[members:]
    columns_ref, gathered, shifted_ref, lse_ref, partial_ref = refs
    mine, place = lax.axis_index("member"), lax.axis_index("dp")
    rows = feats[0].shape[0]
    for k in range(peers):
        chip = mixed(place // 2, k // 2, peers // 2, sender)
        core = lax.bitwise_xor(lax.rem(place, jnp.int32(2)), jnp.int32(k % 2))
        at = chip * 2 + core
        gathered[pl.ds(pl.multiple_of(at * rows, rows), rows), :] = feats[k][...]
    block = columns[0].shape[0]
    for k in range(members):
        at = mixed(mine, k, members, sender)
        columns_ref[pl.ds(pl.multiple_of(at * block, block), block), :] = columns[k][...]
    values = normed(gathered[...], gain_ref[...])
    logits = jnp.dot(values, head_ref[...], preferred_element_type=F32) + bias_ref[...]
    top = jnp.max(logits, axis=1, keepdims=True)
    lse = top + jnp.log(jnp.sum(jnp.exp(logits - top), axis=1, keepdims=True))
    shifted_ref[...] = (logits - lse).astype(BF16)
    lse_ref[...] = jnp.broadcast_to(lse, lse_ref.shape)
    partial_ref[...] = jnp.dot(columns_ref[...], student_ref[...], preferred_element_type=F32)
    classes = logits.shape[1]
    for k in range(members):
        at = pl.ds(pl.multiple_of(mixed(mine, k, members, partner) * block, block), block)
        out = payloads[k]
        out[0:block, :] = shifted_ref[at, :]
        high, middle, _ = split3(partial_ref[at, :])
        out[block : 2 * block, :] = high
        out[2 * block : 3 * block, :] = middle
        lse_row = to_lanes(lse_ref[at, 0:1], classes)
        line = lax.broadcasted_iota(jnp.int32, (PAD, classes), 0)
        high, middle, low = split3(lse_row)
        packed = jnp.where(
            line == 0,
            high.astype(F32),
            jnp.where(line == 1, middle.astype(F32), jnp.where(line == 2, low.astype(F32), 0.0)),
        )
        out[3 * block :, :] = packed.astype(BF16)


def alphas_kernel(members, block, *refs):
    payloads, refs = refs[:members], refs[members:]
    bias_ref, alphas_ref, inner_ref, small_ref = refs
    mine = lax.axis_index("member")
    classes = bias_ref.shape[1]
    target = jnp.zeros((block, classes), F32)
    logits = jnp.zeros((block, classes), F32)
    small_ref[...] = jnp.zeros_like(small_ref)
    lse_total = jnp.zeros((1, LANES), F32)
    for k in range(members):
        got = payloads[k]
        target += got[0:block, :].astype(F32)
        logits += got[block : 2 * block, :].astype(F32) + got[2 * block : 3 * block, :].astype(F32)
        tail = got[3 * block :, 0:LANES].astype(F32)
        lse = tail[0:1, :] + tail[1:2, :] + tail[2:3, :]
        lse_total += lse
        small_ref[pl.ds(mixed(mine, k, members, sender), 1), :] = lse
    target = target * (1.0 / members)
    logits = logits + bias_ref[...]
    alphas = jnp.exp(logits)
    alphas_ref[...] = alphas
    inner_ref[...] = target
    sums = to_lanes(jnp.sum(alphas, axis=1, keepdims=True), LANES)
    parts = to_lanes(
        jnp.sum(log_gamma(alphas, logits) - (alphas - 1.0) * target, axis=1, keepdims=True), LANES
    )
    small_ref[members : members + 1, :] = sums
    small_ref[members + 1 : members + 2, :] = parts - lse_total * (1.0 / members) * (
        sums - float(classes)
    )


def digamma_kernel(alphas_ref, target_ref, inner_ref):
    inner_ref[...] = di_gamma(alphas_ref[...]) - target_ref[...]


def signal_kernel(members, peers, block, *refs):
    smalls, refs = refs[:peers], refs[peers:]
    alphas_ref, inner_ref, signal_ref, held = refs
    place = lax.axis_index("dp")
    for k in range(peers):
        chip = mixed(place // 2, k // 2, peers // 2, sender)
        core = lax.bitwise_xor(lax.rem(place, jnp.int32(2)), jnp.int32(k % 2))
        held[chip * 2 + core] = smalls[k][...]
    everything = held[...]
    classes = alphas_ref.shape[1]
    lse = everything[:, 0:members, :]
    top = jnp.max(lse, axis=0)
    norms = top + jnp.log(jnp.sum(jnp.exp(lse - top[None]), axis=0))
    norm_total = jnp.sum(norms, axis=0, keepdims=True) * (1.0 / members)
    own = jnp.sum(smalls[0][0:members, :], axis=0, keepdims=True) * (1.0 / members)
    alpha_sum = jnp.sum(everything[:, members, :], axis=0, keepdims=True)
    parts = jnp.sum(everything[:, members + 1, :], axis=0, keepdims=True)
    used = lax.broadcasted_iota(jnp.int32, (1, LANES), 1) < block
    alpha_sum = jnp.where(used, alpha_sum, 1.0)
    own_part = (
        parts
        - log_gamma(alpha_sum, jnp.log(alpha_sum))
        + norm_total * (alpha_sum - float(classes * peers))
    )
    loss = jnp.sum(jnp.where(used, own_part, 0.0), axis=1, keepdims=True)
    shift = to_column(di_gamma(alpha_sum) + own - norm_total, block)
    signal_ref[0:block, :] = (alphas_ref[...] * (inner_ref[...] - shift)).astype(BF16)
    line = lax.broadcasted_iota(jnp.int32, (PAD, classes), 0)
    high, middle, low = split3(loss)
    packed = jnp.where(
        line == 0,
        high.astype(F32),
        jnp.where(line == 1, middle.astype(F32), jnp.where(line == 2, low.astype(F32), 0.0)),
    )
    signal_ref[block:, :] = packed.astype(BF16)


def gradient_kernel(members, peers, block, *refs):
    signals, refs = refs[:members], refs[members:]
    columns_ref, loss_ref, grad_ref, bias_ref, held, losses = refs
    mine = lax.axis_index("member")
    images = members * block
    classes = bias_ref.shape[1]
    for k in range(members):
        at = mixed(mine, k, members, sender)
        held[pl.ds(pl.multiple_of(at * block, block), block), :] = signals[k][0:block, :]
        tail = signals[k][block:, 0:LANES].astype(F32)
        losses[pl.ds(at, 1), :] = tail[0:1, :] + tail[1:2, :] + tail[2:3, :]
    signal = held[...]
    grad = lax.dot_general(
        columns_ref[...], signal, (((0,), (0,)), ((), ())), preferred_element_type=F32
    )
    grad_ref[...] = grad * (1.0 / images)
    bias_ref[...] = jnp.sum(signal.astype(F32), axis=0, keepdims=True) * (1.0 / images)
    loss_ref[0, 0] = jnp.sum(losses[:, 0:1]) * (1.0 / (images * classes * peers))


def call(kernel, out_shape, scratch=(), out_specs=None):
    extra = {} if out_specs is None else {"out_specs": out_specs}
    return pl.pallas_call(
        kernel,
        out_shape=out_shape,
        scratch_shapes=list(scratch),
        compiler_params=pltpu.CompilerParams(vmem_limit_bytes=48 * 1024 * 1024),
        **extra,
    )


def on_device(
    teacher_feats,
    teacher_gain,
    teacher_head,
    teacher_bias,
    student_feats,
    student_gain,
    student_head,
    student_bias,
):
    members, peers = lax.axis_size("member"), lax.axis_size("dp")
    shape = jax.ShapeDtypeStruct
    feats = teacher_feats[0]
    rows, depth = feats.shape
    block = student_feats.shape[0]
    images = rows * peers
    width, classes = student_head.shape
    small_rows = -(-(members + 2) // 8) * 8

    chips = [feats] + [send(feats, "dp", k, 2) for k in range(1, peers // 2)]
    pieces = call(
        functools.partial(student_rows, members),
        [shape((block, width), BF16)] * members,
        [pltpu.VMEM((block, depth), BF16)],
    )(student_feats, student_gain[None])
    columns = [pieces[0]] + [send(pieces[k], "member", k) for k in range(1, members)]
    gathered = [part for chip in chips for part in (chip, swap_cores(chip, "dp"))]
    outs = call(
        functools.partial(logits_kernel, members, peers),
        [shape((3 * block + PAD, classes), BF16)] * members + [shape((images, width), BF16)],
        [
            pltpu.VMEM((images, depth), BF16),
            pltpu.VMEM((images, classes), BF16),
            pltpu.VMEM((images, LANES), F32),
            pltpu.VMEM((images, classes), F32),
        ],
    )(*gathered, teacher_gain, teacher_head[0], teacher_bias, *columns, student_head)
    payloads, own_columns = outs[:members], outs[members]
    got = [payloads[0]] + [send(payloads[k], "member", k) for k in range(1, members)]
    alphas, target, small = call(
        functools.partial(alphas_kernel, members, block),
        [shape((block, classes), F32)] * 2 + [shape((small_rows, LANES), F32)],
    )(*got, student_bias[None])
    chips = [small] + [send(small, "dp", k, 2) for k in range(1, peers // 2)]
    inner = call(digamma_kernel, shape((block, classes), F32))(alphas, target)
    smalls = [part for chip in chips for part in (chip, swap_cores(chip, "dp"))]
    signal = call(
        functools.partial(signal_kernel, members, peers, block),
        shape((block + PAD, classes), BF16),
        [pltpu.VMEM((peers, small_rows, LANES), F32)],
    )(*smalls, alphas, inner)
    signals = [signal] + [send(signal, "member", k) for k in range(1, members)]
    loss, head_grad, bias_grad = call(
        functools.partial(gradient_kernel, members, peers, block),
        [shape((1, 1), F32), shape((width, classes), F32), shape((1, classes), F32)],
        [pltpu.VMEM((images, classes), BF16), pltpu.VMEM((members, LANES), F32)],
        [
            pl.BlockSpec(memory_space=pltpu.SMEM),
            pl.BlockSpec(memory_space=pltpu.VMEM),
            pl.BlockSpec(memory_space=pltpu.VMEM),
        ],
    )(*signals, own_columns)
    return (loss[0, 0], head_grad, bias_grad[0])


def solution(mesh):
    placed = (
        P("member", "dp", None),
        P("member", None),
        P("member", None, "dp"),
        P("member", "dp"),
        P("member", None),
        P(),
        P("member", "dp"),
        P("dp"),
    )
    return jax.shard_map(
        on_device,
        mesh=mesh,
        in_specs=placed,
        out_specs=(P(), P("member", "dp"), P("dp")),
        check_vma=False,
    )
```

```python
import functools
import math

import jax
import jax.numpy as jnp
from jax import lax
from jax.experimental import pallas as pl
from jax.experimental.pallas import tpu as pltpu
from jax.sharding import PartitionSpec as P

BF16, F32 = jnp.bfloat16, jnp.float32
LANES = 128
PAD = 16
LANCZOS = (
    0.99999999999980993227684700473478,
    676.520368121885098567009190444019,
    -1259.13921672240287047156078755283,
    771.3234287776530788486528258894,
    -176.61502916214059906584551354,
    12.507343278686904814458936853,
    -0.13857109526572011689554707,
    9.984369578019570859563e-6,
    1.50563273514931155834e-7,
)


def partner(index, k, size):
    return index ^ k if size & (size - 1) == 0 else (index + k) % size


def sender(index, k, size):
    return index ^ k if size & (size - 1) == 0 else (index - k + size) % size


def mixed(index, k, size, of):
    if size & (size - 1) == 0:
        return lax.bitwise_xor(index, jnp.int32(k))
    step = k if of is partner else size - k
    return lax.rem(index + jnp.int32(step), jnp.int32(size))


def send(value, axis, k, scale=1, groups=1):
    size = lax.axis_size(axis) // scale
    pairs = [
        (outer * scale + inner, partner(outer, k, size) * scale + inner)
        for outer in range(size)
        for inner in range(scale)
    ]
    return lax.ppermute(value, axis, pairs)


def swap_cores(value, axis):
    return lax.ppermute(value, axis, [(i, i ^ 1) for i in range(lax.axis_size(axis))])


def normed(values, gain_row):
    values = values.astype(F32)
    center = values - jnp.mean(values, axis=-1, keepdims=True)
    spread = jnp.mean(center * center, axis=-1, keepdims=True)
    return (center * lax.rsqrt(spread + 1e-06) * gain_row).astype(BF16)


def split3(value):
    high = value.astype(BF16)
    rest = value - high.astype(F32)
    middle = rest.astype(BF16)
    return high, middle, (rest - middle.astype(F32)).astype(BF16)


def diagonal(rows, lanes):
    return lax.broadcasted_iota(jnp.int32, (rows, lanes), 0) == lax.broadcasted_iota(
        jnp.int32, (rows, lanes), 1
    )


def to_lanes(column, lanes):
    return jnp.sum(
        jnp.where(diagonal(column.shape[0], lanes), column, 0.0), axis=0, keepdims=True
    )


def to_column(row, rows):
    return jnp.sum(jnp.where(diagonal(rows, row.shape[1]), row, 0.0), axis=1, keepdims=True)


def series(x):
    total = jnp.full_like(x, LANCZOS[0])
    slope = jnp.zeros_like(x)
    for k in range(1, 9):
        inverse = 1.0 / (x + float(k))
        term = LANCZOS[k] * inverse
        total = total + term
        slope = slope - term * inverse
    log_t = math.log(7.5) + jnp.log1p(x / 7.5)
    return total, slope, log_t


def log_gamma(x, log_x):
    total, _, log_t = series(x)
    t = x + 7.5
    return (
        (x + 0.5 - t / log_t) * log_t
        + 0.5 * math.log(2.0 * math.pi)
        + jnp.log(total)
        - log_x
    )


def di_gamma(x):
    total, slope, log_t = series(x)
    return log_t + slope / total - 7.0 / (x + 7.5) - 1.0 / x


def fetch_kernel(*refs):
    count = len(refs) // 2
    sources, targets, sems = refs[:count], refs[count : 2 * count], refs[2 * count]
    copies = [
        pltpu.make_async_copy(source, target, sems.at[i])
        for i, (source, target) in enumerate(zip(sources, targets))
    ]
    for copy in copies:
        copy.start()
    for copy in copies:
        copy.wait()


def fetch(*arrays):
    return pl.pallas_call(
        fetch_kernel,
        out_shape=[jax.ShapeDtypeStruct(a.shape, a.dtype) for a in arrays],
        in_specs=[pl.BlockSpec(memory_space=pl.ANY)] * len(arrays),
        out_specs=[pl.BlockSpec(memory_space=pltpu.VMEM)] * len(arrays),
        scratch_shapes=[pltpu.SemaphoreType.DMA((len(arrays),))],
        cost_estimate=pl.CostEstimate(flops=0, bytes_accessed=1 << 22, transcendentals=0),
    )(*arrays)


def logits_kernel(members, peers, *refs):
    feats, refs = refs[:peers], refs[peers:]
    gain_ref, head_ref, bias_ref, refs = refs[0], refs[1], refs[2], refs[3:]
    students, refs = refs[:members], refs[members:]
    student_gain_ref, student_ref, refs = refs[0], refs[1], refs[2:]
    payloads, refs = refs[:members], refs[members:]
    columns_ref, gathered, held, shifted_ref, lse_ref, partial_ref = refs
    mine, place = lax.axis_index("member"), lax.axis_index("dp")
    rows = feats[0].shape[0]
    for k in range(peers):
        chip = mixed(place // 2, k // 2, peers // 2, sender)
        core = lax.bitwise_xor(lax.rem(place, jnp.int32(2)), jnp.int32(k % 2))
        at = chip * 2 + core
        gathered[pl.ds(pl.multiple_of(at * rows, rows), rows), :] = feats[k][...]
    block = students[0].shape[0]
    width = columns_ref.shape[1]
    for k in range(members):
        at = mixed(mine, k, members, sender)
        held[pl.ds(pl.multiple_of(at * block, block), block), :] = normed(
            students[k][...], student_gain_ref[...]
        )
    if width % LANES == 0:
        columns_ref[...] = held[:, pl.ds(pl.multiple_of(mine * width, LANES), width)]
    else:
        for j in range(members):

            @pl.when(mine == j)
            def _(j=j):
                columns_ref[...] = held[:, j * width : (j + 1) * width]

    values = normed(gathered[...], gain_ref[...])
    logits = jnp.dot(values, head_ref[...], preferred_element_type=F32) + bias_ref[...]
    top = jnp.max(logits, axis=1, keepdims=True)
    lse = top + jnp.log(jnp.sum(jnp.exp(logits - top), axis=1, keepdims=True))
    shifted_ref[...] = (logits - lse).astype(BF16)
    lse_ref[...] = jnp.broadcast_to(lse, lse_ref.shape)
    partial_ref[...] = jnp.dot(columns_ref[...], student_ref[...], preferred_element_type=F32)
    classes = logits.shape[1]
    for k in range(members):
        at = pl.ds(pl.multiple_of(mixed(mine, k, members, partner) * block, block), block)
        out = payloads[k]
        out[0:block, :] = shifted_ref[at, :]
        high, middle, _ = split3(partial_ref[at, :])
        out[block : 2 * block, :] = high
        out[2 * block : 3 * block, :] = middle
        lse_row = to_lanes(lse_ref[at, 0:1], classes)
        line = lax.broadcasted_iota(jnp.int32, (PAD, classes), 0)
        high, middle, low = split3(lse_row)
        packed = jnp.where(
            line == 0,
            high.astype(F32),
            jnp.where(line == 1, middle.astype(F32), jnp.where(line == 2, low.astype(F32), 0.0)),
        )
        out[3 * block :, :] = packed.astype(BF16)


def alphas_kernel(members, block, *refs):
    payloads, refs = refs[:members], refs[members:]
    bias_ref, alphas_ref, inner_ref, small_ref = refs
    mine = lax.axis_index("member")
    classes = bias_ref.shape[1]
    target = jnp.zeros((block, classes), F32)
    logits = jnp.zeros((block, classes), F32)
    small_ref[...] = jnp.zeros_like(small_ref)
    lse_total = jnp.zeros((1, LANES), F32)
    for k in range(members):
        got = payloads[k]
        target += got[0:block, :].astype(F32)
        logits += got[block : 2 * block, :].astype(F32) + got[2 * block : 3 * block, :].astype(F32)
        tail = got[3 * block :, 0:LANES].astype(F32)
        lse = tail[0:1, :] + tail[1:2, :] + tail[2:3, :]
        lse_total += lse
        small_ref[pl.ds(mixed(mine, k, members, sender), 1), :] = lse
    target = target * (1.0 / members)
    logits = logits + bias_ref[...]
    alphas = jnp.exp(logits)
    alphas_ref[...] = alphas
    inner_ref[...] = target
    sums = to_lanes(jnp.sum(alphas, axis=1, keepdims=True), LANES)
    parts = to_lanes(
        jnp.sum(log_gamma(alphas, logits) - (alphas - 1.0) * target, axis=1, keepdims=True), LANES
    )
    small_ref[members : members + 1, :] = sums
    small_ref[members + 1 : members + 2, :] = parts - lse_total * (1.0 / members) * (
        sums - float(classes)
    )


def digamma_kernel(alphas_ref, target_ref, inner_ref):
    inner_ref[...] = di_gamma(alphas_ref[...]) - target_ref[...]


def signal_kernel(members, peers, block, *refs):
    smalls, refs = refs[:peers], refs[peers:]
    alphas_ref, inner_ref, signal_ref, held = refs
    place = lax.axis_index("dp")
    for k in range(peers):
        chip = mixed(place // 2, k // 2, peers // 2, sender)
        core = lax.bitwise_xor(lax.rem(place, jnp.int32(2)), jnp.int32(k % 2))
        held[chip * 2 + core] = smalls[k][...]
    everything = held[...]
    classes = alphas_ref.shape[1]
    lse = everything[:, 0:members, :]
    top = jnp.max(lse, axis=0)
    norms = top + jnp.log(jnp.sum(jnp.exp(lse - top[None]), axis=0))
    norm_total = jnp.sum(norms, axis=0, keepdims=True) * (1.0 / members)
    own = jnp.sum(smalls[0][0:members, :], axis=0, keepdims=True) * (1.0 / members)
    alpha_sum = jnp.sum(everything[:, members, :], axis=0, keepdims=True)
    parts = jnp.sum(everything[:, members + 1, :], axis=0, keepdims=True)
    used = lax.broadcasted_iota(jnp.int32, (1, LANES), 1) < block
    alpha_sum = jnp.where(used, alpha_sum, 1.0)
    own_part = (
        parts
        - log_gamma(alpha_sum, jnp.log(alpha_sum))
        + norm_total * (alpha_sum - float(classes * peers))
    )
    loss = jnp.sum(jnp.where(used, own_part, 0.0), axis=1, keepdims=True)
    shift = to_column(di_gamma(alpha_sum) + own - norm_total, block)
    signal_ref[0:block, :] = (alphas_ref[...] * (inner_ref[...] - shift)).astype(BF16)
    line = lax.broadcasted_iota(jnp.int32, (PAD, classes), 0)
    high, middle, low = split3(loss)
    packed = jnp.where(
        line == 0,
        high.astype(F32),
        jnp.where(line == 1, middle.astype(F32), jnp.where(line == 2, low.astype(F32), 0.0)),
    )
    signal_ref[block:, :] = packed.astype(BF16)


def gradient_kernel(members, peers, block, *refs):
    signals, refs = refs[:members], refs[members:]
    columns_ref, loss_ref, grad_ref, bias_ref, held, losses = refs
    mine = lax.axis_index("member")
    images = members * block
    classes = bias_ref.shape[1]
    for k in range(members):
        at = mixed(mine, k, members, sender)
        held[pl.ds(pl.multiple_of(at * block, block), block), :] = signals[k][0:block, :]
        tail = signals[k][block:, 0:LANES].astype(F32)
        losses[pl.ds(at, 1), :] = tail[0:1, :] + tail[1:2, :] + tail[2:3, :]
    signal = held[...]
    grad = lax.dot_general(
        columns_ref[...], signal, (((0,), (0,)), ((), ())), preferred_element_type=F32
    )
    grad_ref[...] = grad * (1.0 / images)
    bias_ref[...] = jnp.sum(signal.astype(F32), axis=0, keepdims=True) * (1.0 / images)
    loss_ref[0, 0] = jnp.sum(losses[:, 0:1]) * (1.0 / (images * classes * peers))


def call(kernel, out_shape, scratch=(), out_specs=None):
    extra = {} if out_specs is None else {"out_specs": out_specs}
    return pl.pallas_call(
        kernel,
        out_shape=out_shape,
        scratch_shapes=list(scratch),
        compiler_params=pltpu.CompilerParams(vmem_limit_bytes=48 * 1024 * 1024),
        **extra,
    )


def on_device(
    teacher_feats,
    teacher_gain,
    teacher_head,
    teacher_bias,
    student_feats,
    student_gain,
    student_head,
    student_bias,
):
    members, peers = lax.axis_size("member"), lax.axis_size("dp")
    shape = jax.ShapeDtypeStruct
    feats = teacher_feats[0]
    rows, depth = feats.shape
    block = student_feats.shape[0]
    images = rows * peers
    width, classes = student_head.shape
    small_rows = -(-(members + 2) // 8) * 8

    chips = [feats] + [send(feats, "dp", k, 2) for k in range(1, peers // 2)]
    students = [student_feats] + [
        send(student_feats, "member", k) for k in reversed(range(1, members))
    ][::-1]
    head, student_head, *rows_of = fetch(
        teacher_head[0], student_head, teacher_gain, teacher_bias, student_gain[None], student_bias[None]
    )
    teacher_gain, teacher_bias, student_gain, student_bias = rows_of
    gathered = [part for chip in chips for part in (chip, swap_cores(chip, "dp"))]
    outs = call(
        functools.partial(logits_kernel, members, peers),
        [shape((3 * block + PAD, classes), BF16)] * members + [shape((images, width), BF16)],
        [
            pltpu.VMEM((images, depth), BF16),
            pltpu.VMEM((images, depth), BF16),
            pltpu.VMEM((images, classes), BF16),
            pltpu.VMEM((images, LANES), F32),
            pltpu.VMEM((images, classes), F32),
        ],
    )(*gathered, teacher_gain, head, teacher_bias, *students, student_gain, student_head)
    payloads, own_columns = outs[:members], outs[members]
    got = [payloads[0]] + [send(payloads[k], "member", k) for k in range(1, members)]
    alphas, target, small = call(
        functools.partial(alphas_kernel, members, block),
        [shape((block, classes), F32)] * 2 + [shape((small_rows, LANES), F32)],
    )(*got, student_bias)
    chips = [small] + [send(small, "dp", k, 2) for k in range(1, peers // 2)]
    inner = call(digamma_kernel, shape((block, classes), F32))(alphas, target)
    smalls = [part for chip in chips for part in (chip, swap_cores(chip, "dp"))]
    signal = call(
        functools.partial(signal_kernel, members, peers, block),
        shape((block + PAD, classes), BF16),
        [pltpu.VMEM((peers, small_rows, LANES), F32)],
    )(*smalls, alphas, inner)
    signals = [signal] + [send(signal, "member", k) for k in range(1, members)]
    loss, head_grad, bias_grad = call(
        functools.partial(gradient_kernel, members, peers, block),
        [shape((1, 1), F32), shape((width, classes), F32), shape((1, classes), F32)],
        [pltpu.VMEM((images, classes), BF16), pltpu.VMEM((members, LANES), F32)],
        [
            pl.BlockSpec(memory_space=pltpu.SMEM),
            pl.BlockSpec(memory_space=pltpu.VMEM),
            pl.BlockSpec(memory_space=pltpu.VMEM),
        ],
    )(*signals, own_columns)
    return (loss[0, 0], head_grad, bias_grad[0])


def solution(mesh):
    placed = (
        P("member", "dp", None),
        P("member", None),
        P("member", None, "dp"),
        P("member", "dp"),
        P("member", None),
        P(),
        P("member", "dp"),
        P("dp"),
    )
    return jax.shard_map(
        on_device,
        mesh=mesh,
        in_specs=placed,
        out_specs=(P(), P("member", "dp"), P("dp")),
        check_vma=False,
    )
```

```python
import functools
import math

import jax
import jax.numpy as jnp
from jax import lax
from jax.experimental import pallas as pl
from jax.experimental.pallas import tpu as pltpu
from jax.sharding import PartitionSpec as P

BF16, F32 = jnp.bfloat16, jnp.float32
LANES = 128
PAD = 16
LANCZOS = (
    0.99999999999980993227684700473478,
    676.520368121885098567009190444019,
    -1259.13921672240287047156078755283,
    771.3234287776530788486528258894,
    -176.61502916214059906584551354,
    12.507343278686904814458936853,
    -0.13857109526572011689554707,
    9.984369578019570859563e-6,
    1.50563273514931155834e-7,
)


def partner(index, k, size):
    return index ^ k if size & (size - 1) == 0 else (index + k) % size


def sender(index, k, size):
    return index ^ k if size & (size - 1) == 0 else (index - k + size) % size


def mixed(index, k, size, of):
    if size & (size - 1) == 0:
        return lax.bitwise_xor(index, jnp.int32(k))
    step = k if of is partner else size - k
    return lax.rem(index + jnp.int32(step), jnp.int32(size))


def send(value, axis, k, scale=1, groups=1):
    size = lax.axis_size(axis) // scale
    pairs = [
        (outer * scale + inner, partner(outer, k, size) * scale + inner)
        for outer in range(size)
        for inner in range(scale)
    ]
    return lax.ppermute(value, axis, pairs)


def swap_cores(value, axis):
    return lax.ppermute(value, axis, [(i, i ^ 1) for i in range(lax.axis_size(axis))])


def normed(values, gain_row):
    values = values.astype(F32)
    center = values - jnp.mean(values, axis=-1, keepdims=True)
    spread = jnp.mean(center * center, axis=-1, keepdims=True)
    return (center * lax.rsqrt(spread + 1e-06) * gain_row).astype(BF16)


def split3(value):
    high = value.astype(BF16)
    rest = value - high.astype(F32)
    middle = rest.astype(BF16)
    return high, middle, (rest - middle.astype(F32)).astype(BF16)


def diagonal(rows, lanes):
    return lax.broadcasted_iota(jnp.int32, (rows, lanes), 0) == lax.broadcasted_iota(
        jnp.int32, (rows, lanes), 1
    )


def to_lanes(column, lanes):
    return jnp.sum(
        jnp.where(diagonal(column.shape[0], lanes), column, 0.0), axis=0, keepdims=True
    )


def to_column(row, rows):
    return jnp.sum(jnp.where(diagonal(rows, row.shape[1]), row, 0.0), axis=1, keepdims=True)


def series(x):
    total = jnp.full_like(x, LANCZOS[0])
    slope = jnp.zeros_like(x)
    for k in range(1, 9):
        inverse = 1.0 / (x + float(k))
        term = LANCZOS[k] * inverse
        total = total + term
        slope = slope - term * inverse
    log_t = math.log(7.5) + jnp.log1p(x / 7.5)
    return total, slope, log_t


def log_gamma(x, log_x):
    total, _, log_t = series(x)
    t = x + 7.5
    return (
        (x + 0.5 - t / log_t) * log_t
        + 0.5 * math.log(2.0 * math.pi)
        + jnp.log(total)
        - log_x
    )


def di_gamma(x):
    total, slope, log_t = series(x)
    return log_t + slope / total - 7.0 / (x + 7.5) - 1.0 / x


def fetch(sources, targets, sems):
    copies = [
        pltpu.make_async_copy(source, target, sems.at[i])
        for i, (source, target) in enumerate(zip(sources, targets, strict=True))
    ]
    for copy in copies:
        copy.start()
    return copies


def slot(at, rows):
    return pl.ds(pl.multiple_of(at * rows, rows), rows)


def prepare_kernel(other_ref, *refs):
    sources, (pair_ref, own_ref, gain_ref, sems) = refs[:2], refs[2:]
    copies = fetch(sources, (own_ref, gain_ref), sems)
    core = lax.rem(lax.axis_index("dp"), jnp.int32(2))
    rows = other_ref.shape[0]
    for copy in copies:
        copy.wait()
    pair_ref[slot(core, rows), :] = normed(own_ref[...], gain_ref[...])
    pair_ref[slot(1 - core, rows), :] = normed(other_ref[...], gain_ref[...])


def packed3(row, rows, lanes):
    line = lax.broadcasted_iota(jnp.int32, (rows, lanes), 0)
    high, middle, low = (part.astype(F32) for part in split3(row))
    lower = jnp.where(line == 2, low, 0.0)
    return jnp.where(line == 0, high, jnp.where(line == 1, middle, lower)).astype(BF16)


def logits_kernel(members, chips, *refs):
    pairs, refs = refs[:chips], refs[chips:]
    students, refs = refs[: members - 1], refs[members - 1 :]
    sources, refs = refs[:6], refs[6:]
    payloads, refs = refs[:members], refs[members:]
    columns_ref, gathered, held, shifted_ref, lse_ref, partial_ref, *params = refs
    own_ref, gain_ref, head_ref, student_ref, bias_ref, student_bias_ref, sems = params
    copies = fetch(sources, params[:6], sems)
    mine, chip = lax.axis_index("member"), lax.axis_index("dp") // 2
    for k in range(chips):
        at = mixed(chip, k, chips, sender)
        gathered[slot(at, pairs[k].shape[0]), :] = pairs[k][...]
    for copy in copies:
        copy.wait()
    block = own_ref.shape[0]
    width = columns_ref.shape[1]
    for k in range(members):
        source = own_ref if k == 0 else students[k - 1]
        at = slot(mixed(mine, k, members, sender), block)
        held[at, :] = normed(source[...], gain_ref[...])
    if width % LANES == 0:
        columns_ref[...] = held[:, pl.ds(pl.multiple_of(mine * width, LANES), width)]
    else:
        for j in range(members):

            @pl.when(mine == j)
            def _(j=j):
                columns_ref[...] = held[:, j * width : (j + 1) * width]

    logits = jnp.dot(gathered[...], head_ref[...], preferred_element_type=F32) + bias_ref[...]
    top = jnp.max(logits, axis=1, keepdims=True)
    lse = top + jnp.log(jnp.sum(jnp.exp(logits - top), axis=1, keepdims=True))
    shifted_ref[...] = (logits - lse).astype(BF16)
    lse_ref[...] = jnp.broadcast_to(lse, lse_ref.shape)
    partial_ref[...] = jnp.dot(columns_ref[...], student_ref[...], preferred_element_type=F32)
    classes = logits.shape[1]
    for k in range(members):
        at = slot(mixed(mine, k, members, partner), block)
        out = payloads[k]
        out[0:block, :] = shifted_ref[at, :]
        partial = partial_ref[at, :]
        if k == 0:
            partial += student_bias_ref[...][None, :]
        high, middle, _ = split3(partial)
        out[block : 2 * block, :] = high
        out[2 * block : 3 * block, :] = middle
        out[3 * block :, :] = packed3(to_lanes(lse_ref[at, 0:1], classes), PAD, classes)


def alphas_kernel(members, *refs):
    payloads, refs = refs[:members], refs[members:]
    alphas_ref, target_ref, small_ref = refs
    mine = lax.axis_index("member")
    block, classes = alphas_ref.shape
    target = jnp.zeros((block, classes), F32)
    logits = jnp.zeros((block, classes), F32)
    lse_total = jnp.zeros((1, LANES), F32)
    small_ref[...] = jnp.zeros_like(small_ref)
    for k in range(members):
        got = payloads[k]
        target += got[0:block, :].astype(F32)
        logits += got[block : 2 * block, :].astype(F32) + got[2 * block : 3 * block, :].astype(F32)
        tail = got[3 * block :, 0:LANES].astype(F32)
        lse = tail[0:1, :] + tail[1:2, :] + tail[2:3, :]
        lse_total += lse
        small_ref[pl.ds(mixed(mine, k, members, sender), 1), :] = lse
    target = target * (1.0 / members)
    alphas = jnp.exp(logits)
    alphas_ref[...] = alphas
    target_ref[...] = target
    sums = to_lanes(jnp.sum(alphas, axis=1, keepdims=True), LANES)
    parts = to_lanes(
        jnp.sum(log_gamma(alphas, logits) - (alphas - 1.0) * target, axis=1, keepdims=True), LANES
    )
    small_ref[members : members + 1, :] = sums
    small_ref[members + 1 : members + 2, :] = parts - lse_total * (1.0 / members) * (
        sums - float(classes)
    )


def digamma_kernel(alphas_ref, target_ref, inner_ref):
    inner_ref[...] = di_gamma(alphas_ref[...]) - target_ref[...]


def joined(parts, members):
    top = functools.reduce(jnp.maximum, parts)
    logs = top + jnp.log(sum(jnp.exp(part - top) for part in parts))
    line = lax.broadcasted_iota(jnp.int32, top.shape, 0)
    return jnp.where(line < members, logs, sum(parts))


def combine_kernel(members, own_ref, other_ref, out_ref):
    out_ref[...] = joined([own_ref[...], other_ref[...]], members)


def signal_kernel(members, chips, images, classes, *refs):
    smalls, refs = refs[:chips], refs[chips:]
    own_ref, alphas_ref, inner_ref, signal_ref, held = refs
    chip = lax.axis_index("dp") // 2
    block = alphas_ref.shape[0]
    for k in range(chips):
        held[mixed(chip, k, chips, sender)] = smalls[k][...]
    everything = joined([held[k] for k in range(chips)], members)
    norm_total = jnp.sum(everything[0:members, :], axis=0, keepdims=True) * (1.0 / members)
    own = jnp.sum(own_ref[0:members, :], axis=0, keepdims=True) * (1.0 / members)
    used = lax.broadcasted_iota(jnp.int32, (1, LANES), 1) < block
    alpha_sum = jnp.where(used, everything[members : members + 1, :], 1.0)
    shift = to_column(di_gamma(alpha_sum) + own - norm_total, block)
    signal_ref[0:block, :] = (alphas_ref[...] * (inner_ref[...] - shift)).astype(BF16)
    terms = (
        everything[members + 1 : members + 2, :]
        - log_gamma(alpha_sum, jnp.log(alpha_sum))
        + norm_total * (alpha_sum - float(classes))
    )
    loss = jnp.sum(jnp.where(used, terms, 0.0), axis=1, keepdims=True)
    signal_ref[block:, :] = packed3(loss, PAD, alphas_ref.shape[1])


def gradient_kernel(members, images, classes, *refs):
    signals, refs = refs[:members], refs[members:]
    columns_ref, loss_ref, grad_ref, bias_ref, held, losses = refs
    mine = lax.axis_index("member")
    block = images // members
    for k in range(members):
        at = mixed(mine, k, members, sender)
        held[slot(at, block), :] = signals[k][0:block, :]
        tail = signals[k][block:, 0:LANES].astype(F32)
        losses[pl.ds(at, 1), :] = tail[0:1, :] + tail[1:2, :] + tail[2:3, :]
    signal = held[...]
    grad = lax.dot_general(
        columns_ref[...], signal, (((0,), (0,)), ((), ())), preferred_element_type=F32
    )
    grad_ref[...] = grad * (1.0 / images)
    bias_ref[...] = jnp.sum(signal.astype(F32), axis=0) * (1.0 / images)
    loss_ref[0, 0] = jnp.sum(losses[:, 0:1]) * (1.0 / (images * classes))


def call(kernel, out_shape, scratch=(), in_specs=None, out_specs=None):
    extra = {}
    if in_specs is not None:
        extra["in_specs"] = in_specs
    if out_specs is not None:
        extra["out_specs"] = out_specs
    return pl.pallas_call(
        kernel,
        out_shape=out_shape,
        scratch_shapes=list(scratch),
        compiler_params=pltpu.CompilerParams(vmem_limit_bytes=48 * 1024 * 1024),
        **extra,
    )


def on_device(
    teacher_feats,
    teacher_gain,
    teacher_head,
    teacher_bias,
    student_feats,
    student_gain,
    student_head,
    student_bias,
):
    members, peers = lax.axis_size("member"), lax.axis_size("dp")
    chips = peers // 2
    shape = jax.ShapeDtypeStruct
    here, far = pl.BlockSpec(memory_space=pltpu.VMEM), pl.BlockSpec(memory_space=pltpu.HBM)
    feats = teacher_feats[0]
    rows, depth = feats.shape
    block = student_feats.shape[0]
    images = rows * peers
    width, classes = student_head.shape
    small_rows = -(-(members + 2) // 8) * 8

    other = swap_cores(feats, "dp")
    students = [send(student_feats, "member", k) for k in range(1, members)]
    pair = call(
        prepare_kernel,
        shape((2 * rows, depth), BF16),
        [
            pltpu.VMEM((rows, depth), BF16),
            pltpu.VMEM((1, depth), F32),
            pltpu.SemaphoreType.DMA((2,)),
        ],
        [here] + [far] * 2,
    )(other, feats, teacher_gain)
    pairs = [pair] + [send(pair, "dp", k, 2) for k in range(1, chips)]
    *payloads, own_columns = call(
        functools.partial(logits_kernel, members, chips),
        [shape((3 * block + PAD, classes), BF16)] * members + [shape((images, width), BF16)],
        [
            pltpu.VMEM((images, depth), BF16),
            pltpu.VMEM((images, depth), BF16),
            pltpu.VMEM((images, classes), BF16),
            pltpu.VMEM((images, LANES), F32),
            pltpu.VMEM((images, classes), F32),
            pltpu.VMEM((block, depth), BF16),
            pltpu.VMEM((1, depth), F32),
            pltpu.VMEM((depth, classes), BF16),
            pltpu.VMEM((width, classes), BF16),
            pltpu.VMEM((1, classes), F32),
            pltpu.VMEM((classes,), F32),
            pltpu.SemaphoreType.DMA((6,)),
        ],
        [here] * (chips + members - 1) + [far] * 6,
    )(
        *pairs,
        *students,
        student_feats,
        student_gain[None],
        teacher_head[0],
        student_head,
        teacher_bias,
        student_bias,
    )
    got = [payloads[0]] + [send(payloads[k], "member", k) for k in range(1, members)]
    alphas, target, own = call(
        functools.partial(alphas_kernel, members),
        [shape((block, classes), F32)] * 2 + [shape((small_rows, LANES), F32)],
    )(*got)
    other = swap_cores(own, "dp")
    inner = call(digamma_kernel, shape((block, classes), F32))(alphas, target)
    small = call(functools.partial(combine_kernel, members), shape(own.shape, F32))(own, other)
    smalls = [small] + [send(small, "dp", k, 2) for k in range(1, chips)]
    signal = call(
        functools.partial(signal_kernel, members, chips, images, classes * peers),
        shape((block + PAD, classes), BF16),
        [pltpu.VMEM((chips, small_rows, LANES), F32)],
    )(*smalls, own, alphas, inner)
    signals = [signal] + [send(signal, "member", k) for k in range(1, members)]
    loss, head_grad, bias_grad = call(
        functools.partial(gradient_kernel, members, images, classes * peers),
        [shape((1, 1), F32), shape((width, classes), F32), shape((classes,), F32)],
        [pltpu.VMEM((images, classes), BF16), pltpu.VMEM((members, LANES), F32)],
        out_specs=[pl.BlockSpec(memory_space=pltpu.SMEM), here, here],
    )(*signals, own_columns)
    return (loss[0, 0], head_grad, bias_grad)


def solution(mesh):
    placed = (
        P("member", "dp", None),
        P("member", None),
        P("member", None, "dp"),
        P("member", "dp"),
        P("member", None),
        P(),
        P("member", "dp"),
        P("dp"),
    )
    return jax.shard_map(
        on_device,
        mesh=mesh,
        in_specs=placed,
        out_specs=(P(), P("member", "dp"), P("dp")),
        check_vma=False,
    )
```

```python
import functools
import math

import jax
import jax.numpy as jnp
from jax import lax
from jax.experimental import pallas as pl
from jax.experimental.pallas import tpu as pltpu
from jax.sharding import PartitionSpec as P

BF16, F32 = jnp.bfloat16, jnp.float32
LANES = 128
PAD = 16
LANCZOS = (
    0.99999999999980993227684700473478,
    676.520368121885098567009190444019,
    -1259.13921672240287047156078755283,
    771.3234287776530788486528258894,
    -176.61502916214059906584551354,
    12.507343278686904814458936853,
    -0.13857109526572011689554707,
    9.984369578019570859563e-6,
    1.50563273514931155834e-7,
)


def partner(index, k, size):
    return index ^ k if size & (size - 1) == 0 else (index + k) % size


def sender(index, k, size):
    return index ^ k if size & (size - 1) == 0 else (index - k + size) % size


def mixed(index, k, size, of):
    if size & (size - 1) == 0:
        return lax.bitwise_xor(index, jnp.int32(k))
    step = k if of is partner else size - k
    return lax.rem(index + jnp.int32(step), jnp.int32(size))


def send(value, axis, k, scale=1, groups=1):
    size = lax.axis_size(axis) // scale
    pairs = [
        (outer * scale + inner, partner(outer, k, size) * scale + inner)
        for outer in range(size)
        for inner in range(scale)
    ]
    return lax.ppermute(value, axis, pairs)


def swap_cores(value, axis):
    return lax.ppermute(value, axis, [(i, i ^ 1) for i in range(lax.axis_size(axis))])


def normed(values, gain_row):
    values = values.astype(F32)
    center = values - jnp.mean(values, axis=-1, keepdims=True)
    spread = jnp.mean(center * center, axis=-1, keepdims=True)
    return (center * lax.rsqrt(spread + 1e-06) * gain_row).astype(BF16)


def split3(value):
    high = value.astype(BF16)
    rest = value - high.astype(F32)
    middle = rest.astype(BF16)
    return high, middle, (rest - middle.astype(F32)).astype(BF16)


def diagonal(rows, lanes):
    return lax.broadcasted_iota(jnp.int32, (rows, lanes), 0) == lax.broadcasted_iota(
        jnp.int32, (rows, lanes), 1
    )


def to_lanes(column, lanes):
    return jnp.sum(
        jnp.where(diagonal(column.shape[0], lanes), column, 0.0), axis=0, keepdims=True
    )


def to_column(row, rows):
    return jnp.sum(jnp.where(diagonal(rows, row.shape[1]), row, 0.0), axis=1, keepdims=True)


def series(x):
    total = jnp.full_like(x, LANCZOS[0])
    slope = jnp.zeros_like(x)
    for k in range(1, 9):
        inverse = 1.0 / (x + float(k))
        term = LANCZOS[k] * inverse
        total = total + term
        slope = slope - term * inverse
    log_t = math.log(7.5) + jnp.log1p(x / 7.5)
    return total, slope, log_t


def log_gamma(x, log_x):
    total, _, log_t = series(x)
    t = x + 7.5
    return (
        (x + 0.5 - t / log_t) * log_t
        + 0.5 * math.log(2.0 * math.pi)
        + jnp.log(total)
        - log_x
    )


def di_gamma(x):
    total, slope, log_t = series(x)
    return log_t + slope / total - 7.0 / (x + 7.5) - 1.0 / x


def fetch(sources, targets, sems):
    copies = [
        pltpu.make_async_copy(source, target, sems.at[i])
        for i, (source, target) in enumerate(zip(sources, targets, strict=True))
    ]
    for copy in copies:
        copy.start()
    return copies


def slot(at, rows):
    return pl.ds(pl.multiple_of(at * rows, rows), rows)


def first_kernel(out_ref):
    out_ref[...] = jnp.zeros_like(out_ref)


def pair_kernel(own_ref, other_ref, _, pair_ref):
    core = lax.rem(lax.axis_index("dp"), jnp.int32(2))
    rows = own_ref.shape[0]
    pair_ref[slot(core, rows), :] = own_ref[...]
    pair_ref[slot(1 - core, rows), :] = other_ref[...]


def packed3(row, rows, lanes):
    line = lax.broadcasted_iota(jnp.int32, (rows, lanes), 0)
    high, middle, low = (part.astype(F32) for part in split3(row))
    lower = jnp.where(line == 2, low, 0.0)
    return jnp.where(line == 0, high, jnp.where(line == 1, middle, lower)).astype(BF16)


def logits_kernel(members, chips, *refs):
    pairs, refs = refs[:chips], refs[chips:]
    students, refs = refs[: members - 1], refs[members - 1 :]
    sources, refs = refs[:7], refs[7:]
    payloads, refs = refs[:members], refs[members:]
    columns_ref, gathered, held, shifted_ref, lse_ref, partial_ref, *params = refs
    own_ref, student_gain_ref, gain_ref, head_ref, student_ref, bias_ref, student_bias_ref, sems = params
    copies = fetch(sources, params[:7], sems)
    mine, chip = lax.axis_index("member"), lax.axis_index("dp") // 2
    for k in range(chips):
        at = mixed(chip, k, chips, sender)
        gathered[slot(at, pairs[k].shape[0]), :] = pairs[k][...]
    for copy in copies:
        copy.wait()
    block = own_ref.shape[0]
    width = columns_ref.shape[1]
    for k in range(members):
        source = own_ref if k == 0 else students[k - 1]
        at = slot(mixed(mine, k, members, sender), block)
        held[at, :] = normed(source[...], student_gain_ref[...])
    if width % LANES == 0:
        columns_ref[...] = held[:, pl.ds(pl.multiple_of(mine * width, LANES), width)]
    else:
        for j in range(members):

            @pl.when(mine == j)
            def _(j=j):
                columns_ref[...] = held[:, j * width : (j + 1) * width]

    values = normed(gathered[...], gain_ref[...])
    logits = jnp.dot(values, head_ref[...], preferred_element_type=F32) + bias_ref[...]
    top = jnp.max(logits, axis=1, keepdims=True)
    lse = top + jnp.log(jnp.sum(jnp.exp(logits - top), axis=1, keepdims=True))
    shifted_ref[...] = (logits - lse).astype(BF16)
    lse_ref[...] = jnp.broadcast_to(lse, lse_ref.shape)
    partial_ref[...] = jnp.dot(columns_ref[...], student_ref[...], preferred_element_type=F32)
    classes = logits.shape[1]
    for k in range(members):
        at = slot(mixed(mine, k, members, partner), block)
        out = payloads[k]
        out[0:block, :] = shifted_ref[at, :]
        partial = partial_ref[at, :]
        if k == 0:
            partial += student_bias_ref[...][None, :]
        high, middle, _ = split3(partial)
        out[block : 2 * block, :] = high
        out[2 * block : 3 * block, :] = middle
        out[3 * block :, :] = packed3(to_lanes(lse_ref[at, 0:1], classes), PAD, classes)


def alphas_kernel(members, *refs):
    payloads, refs = refs[:members], refs[members:]
    alphas_ref, target_ref, small_ref = refs
    mine = lax.axis_index("member")
    block, classes = alphas_ref.shape
    target = jnp.zeros((block, classes), F32)
    logits = jnp.zeros((block, classes), F32)
    lse_total = jnp.zeros((1, LANES), F32)
    small_ref[...] = jnp.zeros_like(small_ref)
    for k in range(members):
        got = payloads[k]
        target += got[0:block, :].astype(F32)
        logits += got[block : 2 * block, :].astype(F32) + got[2 * block : 3 * block, :].astype(F32)
        tail = got[3 * block :, 0:LANES].astype(F32)
        lse = tail[0:1, :] + tail[1:2, :] + tail[2:3, :]
        lse_total += lse
        small_ref[pl.ds(mixed(mine, k, members, sender), 1), :] = lse
    target = target * (1.0 / members)
    alphas = jnp.exp(logits)
    alphas_ref[...] = alphas
    target_ref[...] = target
    sums = to_lanes(jnp.sum(alphas, axis=1, keepdims=True), LANES)
    parts = to_lanes(
        jnp.sum(log_gamma(alphas, logits) - (alphas - 1.0) * target, axis=1, keepdims=True), LANES
    )
    small_ref[members : members + 1, :] = sums
    small_ref[members + 1 : members + 2, :] = parts - lse_total * (1.0 / members) * (
        sums - float(classes)
    )


def digamma_kernel(alphas_ref, target_ref, inner_ref):
    inner_ref[...] = di_gamma(alphas_ref[...]) - target_ref[...]


def joined(parts, members):
    top = functools.reduce(jnp.maximum, parts)
    logs = top + jnp.log(sum(jnp.exp(part - top) for part in parts))
    line = lax.broadcasted_iota(jnp.int32, top.shape, 0)
    return jnp.where(line < members, logs, sum(parts))


def combine_kernel(members, own_ref, other_ref, out_ref):
    out_ref[...] = joined([own_ref[...], other_ref[...]], members)


def signal_kernel(members, chips, images, classes, *refs):
    smalls, refs = refs[:chips], refs[chips:]
    own_ref, alphas_ref, inner_ref, signal_ref, held = refs
    chip = lax.axis_index("dp") // 2
    block = alphas_ref.shape[0]
    for k in range(chips):
        held[mixed(chip, k, chips, sender)] = smalls[k][...]
    everything = joined([held[k] for k in range(chips)], members)
    norm_total = jnp.sum(everything[0:members, :], axis=0, keepdims=True) * (1.0 / members)
    own = jnp.sum(own_ref[0:members, :], axis=0, keepdims=True) * (1.0 / members)
    used = lax.broadcasted_iota(jnp.int32, (1, LANES), 1) < block
    alpha_sum = jnp.where(used, everything[members : members + 1, :], 1.0)
    shift = to_column(di_gamma(alpha_sum) + own - norm_total, block)
    width = alphas_ref.shape[1]
    signal_ref[:, 0:width] = (alphas_ref[...] * (inner_ref[...] - shift)).astype(BF16)
    terms = (
        everything[members + 1 : members + 2, :]
        - log_gamma(alpha_sum, jnp.log(alpha_sum))
        + norm_total * (alpha_sum - float(classes))
    )
    loss = jnp.sum(jnp.where(used, terms, 0.0), axis=1, keepdims=True)
    signal_ref[:, width:] = packed3(loss, block, LANES)


def gradient_kernel(members, images, classes, *refs):
    signals, refs = refs[:members], refs[members:]
    columns_ref, loss_ref, grad_ref, bias_ref, held, losses = refs
    mine = lax.axis_index("member")
    block = images // members
    width = held.shape[1]
    for k in range(members):
        at = mixed(mine, k, members, sender)
        held[slot(at, block), :] = signals[k][:, 0:width]
        tail = signals[k][:, width:].astype(F32)
        losses[pl.ds(at, 1), :] = tail[0:1, :] + tail[1:2, :] + tail[2:3, :]
    signal = held[...]
    grad = lax.dot_general(
        columns_ref[...], signal, (((0,), (0,)), ((), ())), preferred_element_type=F32
    )
    grad_ref[...] = grad * (1.0 / images)
    bias_ref[...] = jnp.sum(signal.astype(F32), axis=0) * (1.0 / images)
    loss_ref[0, 0] = jnp.sum(losses[:, 0:1]) * (1.0 / (images * classes))


def call(kernel, out_shape, scratch=(), in_specs=None, out_specs=None, flops=0):
    extra = {}
    if flops:
        extra["cost_estimate"] = pl.CostEstimate(flops=flops, bytes_accessed=0, transcendentals=0)
    if in_specs is not None:
        extra["in_specs"] = in_specs
    if out_specs is not None:
        extra["out_specs"] = out_specs
    return pl.pallas_call(
        kernel,
        out_shape=out_shape,
        scratch_shapes=list(scratch),
        compiler_params=pltpu.CompilerParams(vmem_limit_bytes=48 * 1024 * 1024),
        **extra,
    )


def on_device(
    teacher_feats,
    teacher_gain,
    teacher_head,
    teacher_bias,
    student_feats,
    student_gain,
    student_head,
    student_bias,
):
    members, peers = lax.axis_size("member"), lax.axis_size("dp")
    chips = peers // 2
    shape = jax.ShapeDtypeStruct
    here, far = pl.BlockSpec(memory_space=pltpu.VMEM), pl.BlockSpec(memory_space=pltpu.HBM)
    feats = teacher_feats[0]
    rows, depth = feats.shape
    block = student_feats.shape[0]
    images = rows * peers
    width, classes = student_head.shape
    small_rows = -(-(members + 2) // 8) * 8

    other = swap_cores(feats, "dp")
    students = [send(student_feats, "member", k) for k in range(1, members)]
    first = call(first_kernel, shape((8, LANES), F32), flops=1 << 33)()
    pair = call(pair_kernel, shape((2 * rows, depth), BF16), flops=1 << 33)(feats, other, first)
    pairs = [pair] + [send(pair, "dp", k, 2) for k in range(1, chips)]
    *payloads, own_columns = call(
        functools.partial(logits_kernel, members, chips),
        [shape((3 * block + PAD, classes), BF16)] * members + [shape((images, width), BF16)],
        [
            pltpu.VMEM((images, depth), BF16),
            pltpu.VMEM((images, depth), BF16),
            pltpu.VMEM((images, classes), BF16),
            pltpu.VMEM((images, LANES), F32),
            pltpu.VMEM((images, classes), F32),
            pltpu.VMEM((block, depth), BF16),
            pltpu.VMEM((1, depth), F32),
            pltpu.VMEM((1, depth), F32),
            pltpu.VMEM((depth, classes), BF16),
            pltpu.VMEM((width, classes), BF16),
            pltpu.VMEM((1, classes), F32),
            pltpu.VMEM((classes,), F32),
            pltpu.SemaphoreType.DMA((7,)),
        ],
        [here] * (chips + members - 1) + [far] * 7,
    )(
        *pairs,
        *students,
        student_feats,
        student_gain[None],
        teacher_gain,
        teacher_head[0],
        student_head,
        teacher_bias,
        student_bias,
    )
    got = [payloads[0]] + [send(payloads[k], "member", k) for k in range(1, members)]
    alphas, target, own = call(
        functools.partial(alphas_kernel, members),
        [shape((block, classes), F32)] * 2 + [shape((small_rows, LANES), F32)],
    )(*got)
    other = swap_cores(own, "dp")
    inner = call(digamma_kernel, shape((block, classes), F32))(alphas, target)
    small = call(functools.partial(combine_kernel, members), shape(own.shape, F32))(own, other)
    smalls = [small] + [send(small, "dp", k, 2) for k in range(1, chips)]
    signal = call(
        functools.partial(signal_kernel, members, chips, images, classes * peers),
        shape((block, classes + LANES), BF16),
        [pltpu.VMEM((chips, small_rows, LANES), F32)],
    )(*smalls, own, alphas, inner)
    signals = [signal] + [send(signal, "member", k) for k in range(1, members)]
    loss, head_grad, bias_grad = call(
        functools.partial(gradient_kernel, members, images, classes * peers),
        [shape((1, 1), F32), shape((width, classes), F32), shape((classes,), F32)],
        [pltpu.VMEM((images, classes), BF16), pltpu.VMEM((members, LANES), F32)],
        out_specs=[pl.BlockSpec(memory_space=pltpu.SMEM), here, here],
    )(*signals, own_columns)
    return (loss[0, 0], head_grad, bias_grad)


def solution(mesh):
    placed = (
        P("member", "dp", None),
        P("member", None),
        P("member", None, "dp"),
        P("member", "dp"),
        P("member", None),
        P(),
        P("member", "dp"),
        P("dp"),
    )
    return jax.shard_map(
        on_device,
        mesh=mesh,
        in_specs=placed,
        out_specs=(P(), P("member", "dp"), P("dp")),
        check_vma=False,
    )
```

```python
import functools
import math

import jax
import jax.numpy as jnp
from jax import lax
from jax.experimental import pallas as pl
from jax.experimental.pallas import tpu as pltpu
from jax.sharding import PartitionSpec as P

BF16, F32 = jnp.bfloat16, jnp.float32
LANES = 128
PAD = 16
LANCZOS = (
    0.99999999999980993227684700473478,
    676.520368121885098567009190444019,
    -1259.13921672240287047156078755283,
    771.3234287776530788486528258894,
    -176.61502916214059906584551354,
    12.507343278686904814458936853,
    -0.13857109526572011689554707,
    9.984369578019570859563e-6,
    1.50563273514931155834e-7,
)


def partner(index, k, size):
    return index ^ k if size & (size - 1) == 0 else (index + k) % size


def sender(index, k, size):
    return index ^ k if size & (size - 1) == 0 else (index - k + size) % size


def mixed(index, k, size, of):
    if size & (size - 1) == 0:
        return lax.bitwise_xor(index, jnp.int32(k) if isinstance(k, int) else k)
    step = k if of is partner else size - k
    return lax.rem(index + step, jnp.int32(size))


def send(value, axis, k, scale=1, groups=1):
    size = lax.axis_size(axis) // scale
    pairs = [
        (outer * scale + inner, partner(outer, k, size) * scale + inner)
        for outer in range(size)
        for inner in range(scale)
    ]
    return lax.ppermute(value, axis, pairs)


def send_split(value, j):
    members, peers = lax.axis_size("member"), lax.axis_size("dp")
    pairs = [
        (m * peers + d, partner(m, 2 * j + 1 + d % 2, members) * peers + d)
        for m in range(members)
        for d in range(peers)
    ]
    return lax.ppermute(value, ("member", "dp"), pairs)


def swap_cores(value, axis):
    return lax.ppermute(value, axis, [(i, i ^ 1) for i in range(lax.axis_size(axis))])


def normed(values, gain_row):
    values = values.astype(F32)
    center = values - jnp.mean(values, axis=-1, keepdims=True)
    spread = jnp.mean(center * center, axis=-1, keepdims=True)
    return (center * lax.rsqrt(spread + 1e-06) * gain_row).astype(BF16)


def split3(value):
    high = value.astype(BF16)
    rest = value - high.astype(F32)
    middle = rest.astype(BF16)
    return high, middle, (rest - middle.astype(F32)).astype(BF16)


def diagonal(rows, lanes):
    return lax.broadcasted_iota(jnp.int32, (rows, lanes), 0) == lax.broadcasted_iota(
        jnp.int32, (rows, lanes), 1
    )


def to_lanes(column, lanes):
    return jnp.sum(
        jnp.where(diagonal(column.shape[0], lanes), column, 0.0), axis=0, keepdims=True
    )


def to_column(row, rows):
    return jnp.sum(jnp.where(diagonal(rows, row.shape[1]), row, 0.0), axis=1, keepdims=True)


def series(x):
    total = jnp.full_like(x, LANCZOS[0])
    slope = jnp.zeros_like(x)
    for k in range(1, 9):
        inverse = 1.0 / (x + float(k))
        term = LANCZOS[k] * inverse
        total = total + term
        slope = slope - term * inverse
    log_t = math.log(7.5) + jnp.log1p(x / 7.5)
    return total, slope, log_t


def log_gamma(x, log_x):
    total, _, log_t = series(x)
    t = x + 7.5
    return (
        (x + 0.5 - t / log_t) * log_t
        + 0.5 * math.log(2.0 * math.pi)
        + jnp.log(total)
        - log_x
    )


def di_gamma(x):
    total, slope, log_t = series(x)
    return log_t + slope / total - 7.0 / (x + 7.5) - 1.0 / x


def fetch(sources, targets, sems):
    copies = [
        pltpu.make_async_copy(source, target, sems.at[i])
        for i, (source, target) in enumerate(zip(sources, targets, strict=True))
    ]
    for copy in copies:
        copy.start()
    return copies


def slot(at, rows):
    return pl.ds(pl.multiple_of(at * rows, rows), rows)


def first_kernel(out_ref):
    out_ref[...] = jnp.zeros_like(out_ref)


def join_kernel(chips, splits, *refs):
    out_ref, parts = refs[-1], refs[: chips + splits]
    chip = lax.axis_index("dp") // 2
    rows = parts[0].shape[0]
    for k in range(chips):
        out_ref[slot(mixed(chip, k, chips, sender), rows), :] = parts[k][...]
    start = chips * rows
    for part in parts[chips:]:
        out_ref[start : start + part.shape[0], :] = part[...]
        start += part.shape[0]


def packed3(row, rows, lanes):
    line = lax.broadcasted_iota(jnp.int32, (rows, lanes), 0)
    high, middle, low = (part.astype(F32) for part in split3(row))
    lower = jnp.where(line == 2, low, 0.0)
    return jnp.where(line == 0, high, jnp.where(line == 1, middle, lower)).astype(BF16)


def logits_kernel(members, rows, *refs):
    own_ref, other_ref, refs = refs[0], refs[1], refs[2:]
    shared, refs = refs[: (members - 1) % 2], refs[(members - 1) % 2 :]
    sources, refs = refs[:7], refs[7:]
    payloads, refs = refs[:members], refs[members:]
    columns_ref, gathered, held, shifted_ref, lse_ref, partial_ref, *params = refs
    feats_ref, student_gain_ref, gain_ref, head_ref, student_ref, bias_ref, student_bias_ref = params[:7]
    copies = fetch(sources, params[:7], params[7])
    mine, place = lax.axis_index("member"), lax.axis_index("dp")
    core = lax.rem(place, jnp.int32(2))
    chips = gathered.shape[0] // (2 * rows)
    for copy in copies:
        copy.wait()
    block = feats_ref.shape[0]
    width = columns_ref.shape[1]
    held[slot(mine, block), :] = normed(feats_ref[...], student_gain_ref[...])
    for source, side in ((own_ref, core), (other_ref, 1 - core)):
        for chip in range(chips):
            at = slot(2 * chip + side, rows)
            gathered[at, :] = normed(source[chip * rows : (chip + 1) * rows, :], gain_ref[...])
        for j in range((members - 1) // 2):
            start = chips * rows + j * block
            at = slot(mixed(mine, 2 * j + 1 + side, members, sender), block)
            held[at, :] = normed(source[start : start + block, :], student_gain_ref[...])
    for part in shared:
        at = slot(mixed(mine, members - 1, members, sender), block)
        held[at, :] = normed(part[...], student_gain_ref[...])
    if width % LANES == 0:
        columns_ref[...] = held[:, pl.ds(pl.multiple_of(mine * width, LANES), width)]
    else:
        for j in range(members):

            @pl.when(mine == j)
            def _(j=j):
                columns_ref[...] = held[:, j * width : (j + 1) * width]

    logits = jnp.dot(gathered[...], head_ref[...], preferred_element_type=F32) + bias_ref[...]
    top = jnp.max(logits, axis=1, keepdims=True)
    lse = top + jnp.log(jnp.sum(jnp.exp(logits - top), axis=1, keepdims=True))
    shifted_ref[...] = (logits - lse).astype(BF16)
    lse_ref[...] = jnp.broadcast_to(lse, lse_ref.shape)
    partial_ref[...] = jnp.dot(columns_ref[...], student_ref[...], preferred_element_type=F32)
    classes = logits.shape[1]
    for k in range(members):
        at = slot(mixed(mine, k, members, partner), block)
        out = payloads[k]
        out[0:block, :] = shifted_ref[at, :]
        partial = partial_ref[at, :]
        if k == 0:
            partial += student_bias_ref[...][None, :]
        high, middle, _ = split3(partial)
        out[block : 2 * block, :] = high
        out[2 * block : 3 * block, :] = middle
        out[3 * block :, :] = packed3(to_lanes(lse_ref[at, 0:1], classes), PAD, classes)


def alphas_kernel(members, *refs):
    payloads, refs = refs[:members], refs[members:]
    alphas_ref, target_ref, small_ref = refs
    mine = lax.axis_index("member")
    block, classes = alphas_ref.shape
    target = jnp.zeros((block, classes), F32)
    logits = jnp.zeros((block, classes), F32)
    lse_total = jnp.zeros((1, LANES), F32)
    small_ref[...] = jnp.zeros_like(small_ref)
    for k in range(members):
        got = payloads[k]
        target += got[0:block, :].astype(F32)
        logits += got[block : 2 * block, :].astype(F32) + got[2 * block : 3 * block, :].astype(F32)
        tail = got[3 * block :, 0:LANES].astype(F32)
        lse = tail[0:1, :] + tail[1:2, :] + tail[2:3, :]
        lse_total += lse
        small_ref[pl.ds(mixed(mine, k, members, sender), 1), :] = lse
    target = target * (1.0 / members)
    alphas = jnp.exp(logits)
    alphas_ref[...] = alphas
    target_ref[...] = target
    sums = to_lanes(jnp.sum(alphas, axis=1, keepdims=True), LANES)
    parts = to_lanes(
        jnp.sum(log_gamma(alphas, logits) - (alphas - 1.0) * target, axis=1, keepdims=True), LANES
    )
    small_ref[members : members + 1, :] = sums
    small_ref[members + 1 : members + 2, :] = parts - lse_total * (1.0 / members) * (
        sums - float(classes)
    )


def digamma_kernel(alphas_ref, target_ref, inner_ref):
    inner_ref[...] = di_gamma(alphas_ref[...]) - target_ref[...]


def joined(parts, members):
    top = functools.reduce(jnp.maximum, parts)
    logs = top + jnp.log(sum(jnp.exp(part - top) for part in parts))
    line = lax.broadcasted_iota(jnp.int32, top.shape, 0)
    return jnp.where(line < members, logs, sum(parts))


def combine_kernel(members, own_ref, other_ref, out_ref):
    out_ref[...] = joined([own_ref[...], other_ref[...]], members)


def signal_kernel(members, chips, images, classes, *refs):
    smalls, refs = refs[:chips], refs[chips:]
    own_ref, alphas_ref, inner_ref, signal_ref, held = refs
    chip = lax.axis_index("dp") // 2
    block = alphas_ref.shape[0]
    for k in range(chips):
        held[mixed(chip, k, chips, sender)] = smalls[k][...]
    everything = joined([held[k] for k in range(chips)], members)
    norm_total = jnp.sum(everything[0:members, :], axis=0, keepdims=True) * (1.0 / members)
    own = jnp.sum(own_ref[0:members, :], axis=0, keepdims=True) * (1.0 / members)
    used = lax.broadcasted_iota(jnp.int32, (1, LANES), 1) < block
    alpha_sum = jnp.where(used, everything[members : members + 1, :], 1.0)
    shift = to_column(di_gamma(alpha_sum) + own - norm_total, block)
    width = alphas_ref.shape[1]
    signal_ref[:, 0:width] = (alphas_ref[...] * (inner_ref[...] - shift)).astype(BF16)
    terms = (
        everything[members + 1 : members + 2, :]
        - log_gamma(alpha_sum, jnp.log(alpha_sum))
        + norm_total * (alpha_sum - float(classes))
    )
    loss = jnp.sum(jnp.where(used, terms, 0.0), axis=1, keepdims=True)
    signal_ref[:, width:] = packed3(loss, block, LANES)


def gradient_kernel(members, images, classes, *refs):
    signals, refs = refs[:members], refs[members:]
    columns_ref, loss_ref, grad_ref, bias_ref, held, losses = refs
    mine = lax.axis_index("member")
    block = images // members
    width = held.shape[1]
    for k in range(members):
        at = mixed(mine, k, members, sender)
        held[slot(at, block), :] = signals[k][:, 0:width]
        tail = signals[k][:, width:].astype(F32)
        losses[pl.ds(at, 1), :] = tail[0:1, :] + tail[1:2, :] + tail[2:3, :]
    signal = held[...]
    grad = lax.dot_general(
        columns_ref[...], signal, (((0,), (0,)), ((), ())), preferred_element_type=F32
    )
    grad_ref[...] = grad * (1.0 / images)
    bias_ref[...] = jnp.sum(signal.astype(F32), axis=0) * (1.0 / images)
    loss_ref[0, 0] = jnp.sum(losses[:, 0:1]) * (1.0 / (images * classes))


def call(kernel, out_shape, scratch=(), in_specs=None, out_specs=None, flops=0):
    extra = {}
    if flops:
        extra["cost_estimate"] = pl.CostEstimate(flops=flops, bytes_accessed=0, transcendentals=0)
    if in_specs is not None:
        extra["in_specs"] = in_specs
    if out_specs is not None:
        extra["out_specs"] = out_specs
    return pl.pallas_call(
        kernel,
        out_shape=out_shape,
        scratch_shapes=list(scratch),
        compiler_params=pltpu.CompilerParams(vmem_limit_bytes=48 * 1024 * 1024),
        **extra,
    )


def on_device(
    teacher_feats,
    teacher_gain,
    teacher_head,
    teacher_bias,
    student_feats,
    student_gain,
    student_head,
    student_bias,
):
    members, peers = lax.axis_size("member"), lax.axis_size("dp")
    chips = peers // 2
    shape = jax.ShapeDtypeStruct
    here, far = pl.BlockSpec(memory_space=pltpu.VMEM), pl.BlockSpec(memory_space=pltpu.HBM)
    feats = teacher_feats[0]
    rows, depth = feats.shape
    block = student_feats.shape[0]
    images = rows * peers
    width, classes = student_head.shape
    small_rows = -(-(members + 2) // 8) * 8

    parts = [feats] + [send(feats, "dp", k, 2) for k in range(1, chips)]
    parts += [send_split(student_feats, j) for j in range((members - 1) // 2)]
    shared = [send(student_feats, "member", members - 1)] * ((members - 1) % 2)
    first = call(first_kernel, shape((8, LANES), F32), flops=1 << 33)()
    own = call(
        functools.partial(join_kernel, chips, (members - 1) // 2),
        shape((chips * rows + (members - 1) // 2 * block, depth), BF16),
        flops=1 << 33,
    )(*parts, *shared, first)
    *payloads, own_columns = call(
        functools.partial(logits_kernel, members, rows),
        [shape((3 * block + PAD, classes), BF16)] * members + [shape((images, width), BF16)],
        [
            pltpu.VMEM((images, depth), BF16),
            pltpu.VMEM((images, depth), BF16),
            pltpu.VMEM((images, classes), BF16),
            pltpu.VMEM((images, LANES), F32),
            pltpu.VMEM((images, classes), F32),
            pltpu.VMEM((block, depth), BF16),
            pltpu.VMEM((1, depth), F32),
            pltpu.VMEM((1, depth), F32),
            pltpu.VMEM((depth, classes), BF16),
            pltpu.VMEM((width, classes), BF16),
            pltpu.VMEM((1, classes), F32),
            pltpu.VMEM((classes,), F32),
            pltpu.SemaphoreType.DMA((7,)),
        ],
        [here] * (2 + len(shared)) + [far] * 7,
    )(
        own,
        swap_cores(own, "dp"),
        *shared,
        student_feats,
        student_gain[None],
        teacher_gain,
        teacher_head[0],
        student_head,
        teacher_bias,
        student_bias,
    )
    got = [payloads[0]] + [send(payloads[k], "member", k) for k in range(1, members)]
    alphas, target, own = call(
        functools.partial(alphas_kernel, members),
        [shape((block, classes), F32)] * 2 + [shape((small_rows, LANES), F32)],
    )(*got)
    other = swap_cores(own, "dp")
    inner = call(digamma_kernel, shape((block, classes), F32))(alphas, target)
    small = call(functools.partial(combine_kernel, members), shape(own.shape, F32))(own, other)
    smalls = [small] + [send(small, "dp", k, 2) for k in range(1, chips)]
    signal = call(
        functools.partial(signal_kernel, members, chips, images, classes * peers),
        shape((block, classes + LANES), BF16),
        [pltpu.VMEM((chips, small_rows, LANES), F32)],
    )(*smalls, own, alphas, inner)
    signals = [signal] + [send(signal, "member", k) for k in range(1, members)]
    loss, head_grad, bias_grad = call(
        functools.partial(gradient_kernel, members, images, classes * peers),
        [shape((1, 1), F32), shape((width, classes), F32), shape((classes,), F32)],
        [pltpu.VMEM((images, classes), BF16), pltpu.VMEM((members, LANES), F32)],
        out_specs=[pl.BlockSpec(memory_space=pltpu.SMEM), here, here],
    )(*signals, own_columns)
    return (loss[0, 0], head_grad, bias_grad)


def solution(mesh):
    placed = (
        P("member", "dp", None),
        P("member", None),
        P("member", None, "dp"),
        P("member", "dp"),
        P("member", None),
        P(),
        P("member", "dp"),
        P("dp"),
    )
    return jax.shard_map(
        on_device,
        mesh=mesh,
        in_specs=placed,
        out_specs=(P(), P("member", "dp"), P("dp")),
        check_vma=False,
    )
```

```python
import functools
import math

import jax
import jax.numpy as jnp
from jax import lax
from jax.experimental import pallas as pl
from jax.experimental.pallas import tpu as pltpu
from jax.sharding import PartitionSpec as P

BF16, F32 = jnp.bfloat16, jnp.float32
LANES = 128
PAD = 16
LANCZOS = (
    0.99999999999980993227684700473478,
    676.520368121885098567009190444019,
    -1259.13921672240287047156078755283,
    771.3234287776530788486528258894,
    -176.61502916214059906584551354,
    12.507343278686904814458936853,
    -0.13857109526572011689554707,
    9.984369578019570859563e-6,
    1.50563273514931155834e-7,
)


def partner(index, k, size):
    return index ^ k if size & (size - 1) == 0 else (index + k) % size


def sender(index, k, size):
    return index ^ k if size & (size - 1) == 0 else (index - k + size) % size


def mixed(index, k, size, of):
    if size & (size - 1) == 0:
        return lax.bitwise_xor(index, jnp.int32(k) if isinstance(k, int) else k)
    step = k if of is partner else size - k
    return lax.rem(index + step, jnp.int32(size))


def send(value, axis, k, scale=1, groups=1):
    size = lax.axis_size(axis) // scale
    pairs = [
        (outer * scale + inner, partner(outer, k, size) * scale + inner)
        for outer in range(size)
        for inner in range(scale)
    ]
    return lax.ppermute(value, axis, pairs)


def split_step(j, core, members):
    return jnp.where(core == 0, 2 * j + 1, 2 * j + 2 if 2 * j + 2 < members else 1)


def send_split(value, j):
    members, peers = lax.axis_size("member"), lax.axis_size("dp")
    steps = 2 * j + 1, (2 * j + 2 if 2 * j + 2 < members else 1)
    pairs = [
        (m * peers + d, partner(m, steps[d % 2], members) * peers + d)
        for m in range(members)
        for d in range(peers)
    ]
    return lax.ppermute(value, ("member", "dp"), pairs)


def swap_cores(value, axis):
    return lax.ppermute(value, axis, [(i, i ^ 1) for i in range(lax.axis_size(axis))])


def normed(values, gain_row):
    values = values.astype(F32)
    center = values - jnp.mean(values, axis=-1, keepdims=True)
    spread = jnp.mean(center * center, axis=-1, keepdims=True)
    return (center * lax.rsqrt(spread + 1e-06) * gain_row).astype(BF16)


def split3(value):
    high = value.astype(BF16)
    rest = value - high.astype(F32)
    middle = rest.astype(BF16)
    return high, middle, (rest - middle.astype(F32)).astype(BF16)


def diagonal(rows, lanes):
    return lax.broadcasted_iota(jnp.int32, (rows, lanes), 0) == lax.broadcasted_iota(
        jnp.int32, (rows, lanes), 1
    )


def to_lanes(column, lanes):
    return jnp.sum(
        jnp.where(diagonal(column.shape[0], lanes), column, 0.0), axis=0, keepdims=True
    )


def to_column(row, rows):
    return jnp.sum(jnp.where(diagonal(rows, row.shape[1]), row, 0.0), axis=1, keepdims=True)


def series(x):
    total = jnp.full_like(x, LANCZOS[0])
    slope = jnp.zeros_like(x)
    for k in range(1, 9):
        inverse = 1.0 / (x + float(k))
        term = LANCZOS[k] * inverse
        total = total + term
        slope = slope - term * inverse
    log_t = math.log(7.5) + jnp.log1p(x / 7.5)
    return total, slope, log_t


def log_gamma(x, log_x):
    total, _, log_t = series(x)
    t = x + 7.5
    return (
        (x + 0.5 - t / log_t) * log_t
        + 0.5 * math.log(2.0 * math.pi)
        + jnp.log(total)
        - log_x
    )


def di_gamma(x):
    total, slope, log_t = series(x)
    return log_t + slope / total - 7.0 / (x + 7.5) - 1.0 / x


def fetch(sources, targets, sems):
    copies = [
        pltpu.make_async_copy(source, target, sems.at[i])
        for i, (source, target) in enumerate(zip(sources, targets, strict=True))
    ]
    for copy in copies:
        copy.start()
    return copies


def slot(at, rows):
    return pl.ds(pl.multiple_of(at * rows, rows), rows)


def first_kernel(out_ref):
    out_ref[...] = jnp.zeros_like(out_ref)


def student_kernel(*refs):
    *parts, gain_ref, _, out_ref = refs
    rows = parts[0].shape[0]
    for j, part in enumerate(parts):
        out_ref[j * rows : (j + 1) * rows, :] = normed(part[...], gain_ref[...])


def join_kernel(chips, *refs):
    *parts, student_ref, out_ref = refs
    chip = lax.axis_index("dp") // 2
    rows = parts[0].shape[0]
    for k in range(chips):
        out_ref[slot(mixed(chip, k, chips, sender), rows), :] = parts[k][...]
    start = chips * rows
    out_ref[start:, :] = student_ref[...]


def packed3(row, rows, lanes):
    line = lax.broadcasted_iota(jnp.int32, (rows, lanes), 0)
    high, middle, low = (part.astype(F32) for part in split3(row))
    lower = jnp.where(line == 2, low, 0.0)
    return jnp.where(line == 0, high, jnp.where(line == 1, middle, lower)).astype(BF16)


def logits_kernel(members, rows, *refs):
    own_ref, other_ref, refs = refs[0], refs[1], refs[2:]
    sources, refs = refs[:7], refs[7:]
    payloads, refs = refs[:members], refs[members:]
    columns_ref, gathered, held, shifted_ref, lse_ref, partial_ref, *params = refs
    feats_ref, student_gain_ref, gain_ref, head_ref, student_ref, bias_ref, student_bias_ref = params[:7]
    copies = fetch(sources, params[:7], params[7])
    mine, place = lax.axis_index("member"), lax.axis_index("dp")
    core = lax.rem(place, jnp.int32(2))
    chips = gathered.shape[0] // (2 * rows)
    for copy in copies:
        copy.wait()
    block = feats_ref.shape[0]
    width = columns_ref.shape[1]
    held[slot(mine, block), :] = normed(feats_ref[...], student_gain_ref[...])
    for source, side in ((own_ref, core), (other_ref, 1 - core)):
        for chip in range(chips):
            at = slot(2 * chip + side, rows)
            gathered[at, :] = normed(source[chip * rows : (chip + 1) * rows, :], gain_ref[...])
        for j in range(members // 2):
            start = chips * rows + j * block
            at = slot(mixed(mine, split_step(j, side, members), members, sender), block)
            held[at, :] = source[start : start + block, :]
    if width % LANES == 0:
        columns_ref[...] = held[:, pl.ds(pl.multiple_of(mine * width, LANES), width)]
    else:
        for j in range(members):

            @pl.when(mine == j)
            def _(j=j):
                columns_ref[...] = held[:, j * width : (j + 1) * width]

    logits = jnp.dot(gathered[...], head_ref[...], preferred_element_type=F32) + bias_ref[...]
    top = jnp.max(logits, axis=1, keepdims=True)
    lse = top + jnp.log(jnp.sum(jnp.exp(logits - top), axis=1, keepdims=True))
    shifted_ref[...] = (logits - lse).astype(BF16)
    lse_ref[...] = jnp.broadcast_to(lse, lse_ref.shape)
    partial_ref[...] = jnp.dot(columns_ref[...], student_ref[...], preferred_element_type=F32)
    classes = logits.shape[1]
    for k in range(members):
        at = slot(mixed(mine, k, members, partner), block)
        out = payloads[k]
        out[0:block, :] = shifted_ref[at, :]
        partial = partial_ref[at, :]
        if k == 0:
            partial += student_bias_ref[...][None, :]
        high, middle, _ = split3(partial)
        out[block : 2 * block, :] = high
        out[2 * block : 3 * block, :] = middle
        out[3 * block :, :] = packed3(to_lanes(lse_ref[at, 0:1], classes), PAD, classes)


def alphas_kernel(members, *refs):
    payloads, refs = refs[:members], refs[members:]
    alphas_ref, target_ref, small_ref = refs
    mine = lax.axis_index("member")
    block, classes = alphas_ref.shape
    target = jnp.zeros((block, classes), F32)
    logits = jnp.zeros((block, classes), F32)
    lse_total = jnp.zeros((1, LANES), F32)
    small_ref[...] = jnp.zeros_like(small_ref)
    for k in range(members):
        got = payloads[k]
        target += got[0:block, :].astype(F32)
        logits += got[block : 2 * block, :].astype(F32) + got[2 * block : 3 * block, :].astype(F32)
        tail = got[3 * block :, 0:LANES].astype(F32)
        lse = tail[0:1, :] + tail[1:2, :] + tail[2:3, :]
        lse_total += lse
        small_ref[pl.ds(mixed(mine, k, members, sender), 1), :] = lse
    target = target * (1.0 / members)
    alphas = jnp.exp(logits)
    alphas_ref[...] = alphas
    target_ref[...] = target
    sums = to_lanes(jnp.sum(alphas, axis=1, keepdims=True), LANES)
    parts = to_lanes(
        jnp.sum(log_gamma(alphas, logits) - (alphas - 1.0) * target, axis=1, keepdims=True), LANES
    )
    small_ref[members : members + 1, :] = sums
    small_ref[members + 1 : members + 2, :] = parts - lse_total * (1.0 / members) * (
        sums - float(classes)
    )


def digamma_kernel(alphas_ref, target_ref, inner_ref):
    inner_ref[...] = di_gamma(alphas_ref[...]) - target_ref[...]


def joined(parts, members):
    top = functools.reduce(jnp.maximum, parts)
    logs = top + jnp.log(sum(jnp.exp(part - top) for part in parts))
    line = lax.broadcasted_iota(jnp.int32, top.shape, 0)
    return jnp.where(line < members, logs, sum(parts))


def combine_kernel(members, own_ref, other_ref, out_ref):
    out_ref[...] = joined([own_ref[...], other_ref[...]], members)


def signal_kernel(members, chips, images, classes, *refs):
    smalls, refs = refs[:chips], refs[chips:]
    own_ref, alphas_ref, inner_ref, signal_ref, held = refs
    chip = lax.axis_index("dp") // 2
    block = alphas_ref.shape[0]
    for k in range(chips):
        held[mixed(chip, k, chips, sender)] = smalls[k][...]
    everything = joined([held[k] for k in range(chips)], members)
    norm_total = jnp.sum(everything[0:members, :], axis=0, keepdims=True) * (1.0 / members)
    own = jnp.sum(own_ref[0:members, :], axis=0, keepdims=True) * (1.0 / members)
    used = lax.broadcasted_iota(jnp.int32, (1, LANES), 1) < block
    alpha_sum = jnp.where(used, everything[members : members + 1, :], 1.0)
    shift = to_column(di_gamma(alpha_sum) + own - norm_total, block)
    width = alphas_ref.shape[1]
    signal_ref[:, 0:width] = (alphas_ref[...] * (inner_ref[...] - shift)).astype(BF16)
    terms = (
        everything[members + 1 : members + 2, :]
        - log_gamma(alpha_sum, jnp.log(alpha_sum))
        + norm_total * (alpha_sum - float(classes))
    )
    loss = jnp.sum(jnp.where(used, terms, 0.0), axis=1, keepdims=True)
    signal_ref[:, width:] = packed3(loss, block, LANES)


def gradient_kernel(members, images, classes, *refs):
    signals, refs = refs[:members], refs[members:]
    columns_ref, loss_ref, grad_ref, bias_ref, held, losses = refs
    mine = lax.axis_index("member")
    block = images // members
    width = held.shape[1]
    for k in range(members):
        at = mixed(mine, k, members, sender)
        held[slot(at, block), :] = signals[k][:, 0:width]
        tail = signals[k][:, width:].astype(F32)
        losses[pl.ds(at, 1), :] = tail[0:1, :] + tail[1:2, :] + tail[2:3, :]
    signal = held[...]
    grad = lax.dot_general(
        columns_ref[...], signal, (((0,), (0,)), ((), ())), preferred_element_type=F32
    )
    grad_ref[...] = grad * (1.0 / images)
    bias_ref[...] = jnp.sum(signal.astype(F32), axis=0) * (1.0 / images)
    loss_ref[0, 0] = jnp.sum(losses[:, 0:1]) * (1.0 / (images * classes))


def call(kernel, out_shape, scratch=(), in_specs=None, out_specs=None, flops=0):
    extra = {}
    if flops:
        extra["cost_estimate"] = pl.CostEstimate(flops=flops, bytes_accessed=0, transcendentals=0)
    if in_specs is not None:
        extra["in_specs"] = in_specs
    if out_specs is not None:
        extra["out_specs"] = out_specs
    return pl.pallas_call(
        kernel,
        out_shape=out_shape,
        scratch_shapes=list(scratch),
        compiler_params=pltpu.CompilerParams(vmem_limit_bytes=48 * 1024 * 1024),
        **extra,
    )


def on_device(
    teacher_feats,
    teacher_gain,
    teacher_head,
    teacher_bias,
    student_feats,
    student_gain,
    student_head,
    student_bias,
):
    members, peers = lax.axis_size("member"), lax.axis_size("dp")
    chips = peers // 2
    shape = jax.ShapeDtypeStruct
    here, far = pl.BlockSpec(memory_space=pltpu.VMEM), pl.BlockSpec(memory_space=pltpu.HBM)
    feats = teacher_feats[0]
    rows, depth = feats.shape
    block = student_feats.shape[0]
    images = rows * peers
    width, classes = student_head.shape
    small_rows = -(-(members + 2) // 8) * 8

    first = call(first_kernel, shape((8, LANES), F32), flops=1 << 28)()
    students = call(
        student_kernel, shape((members // 2 * block, depth), BF16), flops=1 << 33
    )(*[send_split(student_feats, j) for j in range(members // 2)], student_gain[None], first)
    parts = [feats] + [send(feats, "dp", k, 2) for k in range(1, chips)]
    own = call(
        functools.partial(join_kernel, chips),
        shape((chips * rows + members // 2 * block, depth), BF16),
        flops=1 << 33,
    )(*parts, students)
    *payloads, own_columns = call(
        functools.partial(logits_kernel, members, rows),
        [shape((3 * block + PAD, classes), BF16)] * members + [shape((images, width), BF16)],
        [
            pltpu.VMEM((images, depth), BF16),
            pltpu.VMEM((images, depth), BF16),
            pltpu.VMEM((images, classes), BF16),
            pltpu.VMEM((images, LANES), F32),
            pltpu.VMEM((images, classes), F32),
            pltpu.VMEM((block, depth), BF16),
            pltpu.VMEM((1, depth), F32),
            pltpu.VMEM((1, depth), F32),
            pltpu.VMEM((depth, classes), BF16),
            pltpu.VMEM((width, classes), BF16),
            pltpu.VMEM((1, classes), F32),
            pltpu.VMEM((classes,), F32),
            pltpu.SemaphoreType.DMA((7,)),
        ],
        [here] * 2 + [far] * 7,
    )(
        own,
        swap_cores(own, "dp"),
        student_feats,
        student_gain[None],
        teacher_gain,
        teacher_head[0],
        student_head,
        teacher_bias,
        student_bias,
    )
    got = [payloads[0]] + [send(payloads[k], "member", k) for k in range(1, members)]
    alphas, target, own = call(
        functools.partial(alphas_kernel, members),
        [shape((block, classes), F32)] * 2 + [shape((small_rows, LANES), F32)],
    )(*got)
    other = swap_cores(own, "dp")
    inner = call(digamma_kernel, shape((block, classes), F32))(alphas, target)
    small = call(functools.partial(combine_kernel, members), shape(own.shape, F32))(own, other)
    smalls = [small] + [send(small, "dp", k, 2) for k in range(1, chips)]
    signal = call(
        functools.partial(signal_kernel, members, chips, images, classes * peers),
        shape((block, classes + LANES), BF16),
        [pltpu.VMEM((chips, small_rows, LANES), F32)],
    )(*smalls, own, alphas, inner)
    signals = [signal] + [send(signal, "member", k) for k in range(1, members)]
    loss, head_grad, bias_grad = call(
        functools.partial(gradient_kernel, members, images, classes * peers),
        [shape((1, 1), F32), shape((width, classes), F32), shape((classes,), F32)],
        [pltpu.VMEM((images, classes), BF16), pltpu.VMEM((members, LANES), F32)],
        out_specs=[pl.BlockSpec(memory_space=pltpu.SMEM), here, here],
    )(*signals, own_columns)
    return (loss[0, 0], head_grad, bias_grad)


def solution(mesh):
    placed = (
        P("member", "dp", None),
        P("member", None),
        P("member", None, "dp"),
        P("member", "dp"),
        P("member", None),
        P(),
        P("member", "dp"),
        P("dp"),
    )
    return jax.shard_map(
        on_device,
        mesh=mesh,
        in_specs=placed,
        out_specs=(P(), P("member", "dp"), P("dp")),
        check_vma=False,
    )
```

```python
import functools
import math

import jax
import jax.numpy as jnp
from jax import lax
from jax.experimental import pallas as pl
from jax.experimental.pallas import tpu as pltpu
from jax.sharding import PartitionSpec as P

BF16, F32 = jnp.bfloat16, jnp.float32
LANES = 128
PAD = 16
LANCZOS = (
    0.99999999999980993227684700473478,
    676.520368121885098567009190444019,
    -1259.13921672240287047156078755283,
    771.3234287776530788486528258894,
    -176.61502916214059906584551354,
    12.507343278686904814458936853,
    -0.13857109526572011689554707,
    9.984369578019570859563e-6,
    1.50563273514931155834e-7,
)


def partner(index, k, size):
    return index ^ k if size & (size - 1) == 0 else (index + k) % size


def sender(index, k, size):
    return index ^ k if size & (size - 1) == 0 else (index - k + size) % size


def mixed(index, k, size, of):
    if size & (size - 1) == 0:
        return lax.bitwise_xor(index, jnp.int32(k) if isinstance(k, int) else k)
    step = k if of is partner else size - k
    return lax.rem(index + step, jnp.int32(size))


def send(value, axis, k, scale=1, groups=1):
    size = lax.axis_size(axis) // scale
    pairs = [
        (outer * scale + inner, partner(outer, k, size) * scale + inner)
        for outer in range(size)
        for inner in range(scale)
    ]
    return lax.ppermute(value, axis, pairs)


def split_step(j, core, members):
    return jnp.where(core == 0, 2 * j + 1, 2 * j + 2 if 2 * j + 2 < members else 1)


def send_split(value, j):
    members, peers = lax.axis_size("member"), lax.axis_size("dp")
    steps = 2 * j + 1, (2 * j + 2 if 2 * j + 2 < members else 1)
    pairs = [
        (m * peers + d, partner(m, steps[d % 2], members) * peers + d)
        for m in range(members)
        for d in range(peers)
    ]
    return lax.ppermute(value, ("member", "dp"), pairs)


def swap_cores(value, axis):
    return lax.ppermute(value, axis, [(i, i ^ 1) for i in range(lax.axis_size(axis))])


def normed(values, gain_row):
    values = values.astype(F32)
    center = values - jnp.mean(values, axis=-1, keepdims=True)
    spread = jnp.mean(center * center, axis=-1, keepdims=True)
    return (center * lax.rsqrt(spread + 1e-06) * gain_row).astype(BF16)


def split3(value):
    high = value.astype(BF16)
    rest = value - high.astype(F32)
    middle = rest.astype(BF16)
    return high, middle, (rest - middle.astype(F32)).astype(BF16)


def diagonal(rows, lanes):
    return lax.broadcasted_iota(jnp.int32, (rows, lanes), 0) == lax.broadcasted_iota(
        jnp.int32, (rows, lanes), 1
    )


def to_lanes(column, lanes):
    return jnp.sum(
        jnp.where(diagonal(column.shape[0], lanes), column, 0.0), axis=0, keepdims=True
    )


def to_column(row, rows):
    return jnp.sum(jnp.where(diagonal(rows, row.shape[1]), row, 0.0), axis=1, keepdims=True)


def series(x):
    total = jnp.full_like(x, LANCZOS[0])
    slope = jnp.zeros_like(x)
    for k in range(1, 9):
        inverse = 1.0 / (x + float(k))
        term = LANCZOS[k] * inverse
        total = total + term
        slope = slope - term * inverse
    log_t = math.log(7.5) + jnp.log1p(x / 7.5)
    return total, slope, log_t


def log_gamma(x, log_x):
    total, _, log_t = series(x)
    t = x + 7.5
    return (
        (x + 0.5 - t / log_t) * log_t
        + 0.5 * math.log(2.0 * math.pi)
        + jnp.log(total)
        - log_x
    )


def di_gamma(x):
    total, slope, log_t = series(x)
    return log_t + slope / total - 7.0 / (x + 7.5) - 1.0 / x


def fetch(sources, targets, sems):
    copies = [
        pltpu.make_async_copy(source, target, sems.at[i])
        for i, (source, target) in enumerate(zip(sources, targets, strict=True))
    ]
    for copy in copies:
        copy.start()
    return copies


def slot(at, rows):
    return pl.ds(pl.multiple_of(at * rows, rows), rows)


def first_kernel(out_ref):
    out_ref[...] = jnp.zeros_like(out_ref)


def student_kernel(*refs):
    *parts, gain_ref, _, out_ref = refs
    rows = parts[0].shape[0]
    for j, part in enumerate(parts):
        out_ref[j * rows : (j + 1) * rows, :] = normed(part[...], gain_ref[...])


def join_kernel(chips, *refs):
    *parts, student_ref, out_ref = refs
    chip = lax.axis_index("dp") // 2
    rows = parts[0].shape[0]
    for k in range(chips):
        out_ref[slot(mixed(chip, k, chips, sender), rows), :] = parts[k][...]
    start = chips * rows
    out_ref[start:, :] = student_ref[...]


def packed3(row, rows, lanes):
    line = lax.broadcasted_iota(jnp.int32, (rows, lanes), 0)
    high, middle, low = (part.astype(F32) for part in split3(row))
    lower = jnp.where(line == 2, low, 0.0)
    return jnp.where(line == 0, high, jnp.where(line == 1, middle, lower)).astype(BF16)


def logits_kernel(members, rows, *refs):
    own_ref, other_ref, refs = refs[0], refs[1], refs[2:]
    sources, refs = refs[:7], refs[7:]
    payloads, refs = refs[:members], refs[members:]
    own_logits_ref, columns_ref, gathered, held, shifted_ref, lse_ref, partial_ref, *params = refs
    feats_ref, student_gain_ref, gain_ref, head_ref, student_ref, bias_ref, student_bias_ref = params[:7]
    copies = fetch(sources, params[:7], params[7])
    mine, place = lax.axis_index("member"), lax.axis_index("dp")
    core = lax.rem(place, jnp.int32(2))
    chips = gathered.shape[0] // (2 * rows)
    for copy in copies:
        copy.wait()
    block = feats_ref.shape[0]
    width = columns_ref.shape[1]
    held[slot(mine, block), :] = normed(feats_ref[...], student_gain_ref[...])
    for source, side in ((own_ref, core), (other_ref, 1 - core)):
        for chip in range(chips):
            at = slot(2 * chip + side, rows)
            gathered[at, :] = normed(source[chip * rows : (chip + 1) * rows, :], gain_ref[...])
        for j in range(members // 2):
            start = chips * rows + j * block
            at = slot(mixed(mine, split_step(j, side, members), members, sender), block)
            held[at, :] = source[start : start + block, :]
    if width % LANES == 0:
        columns_ref[...] = held[:, pl.ds(pl.multiple_of(mine * width, LANES), width)]
    else:
        for j in range(members):

            @pl.when(mine == j)
            def _(j=j):
                columns_ref[...] = held[:, j * width : (j + 1) * width]

    logits = jnp.dot(gathered[...], head_ref[...], preferred_element_type=F32) + bias_ref[...]
    top = jnp.max(logits, axis=1, keepdims=True)
    lse = top + jnp.log(jnp.sum(jnp.exp(logits - top), axis=1, keepdims=True))
    shifted_ref[...] = (logits - lse).astype(BF16)
    lse_ref[...] = jnp.broadcast_to(lse, lse_ref.shape)
    partial_ref[...] = jnp.dot(columns_ref[...], student_ref[...], preferred_element_type=F32)
    classes = logits.shape[1]
    for k in range(members):
        at = slot(mixed(mine, k, members, partner), block)
        out = payloads[k]
        out[0:block, :] = shifted_ref[at, :]
        if k == 0:
            own_logits_ref[...] = partial_ref[at, :] + student_bias_ref[...][None, :]
        out[block : 2 * block, :] = partial_ref[at, :].astype(BF16)
        out[2 * block :, :] = packed3(to_lanes(lse_ref[at, 0:1], classes), PAD, classes)


def alphas_kernel(members, *refs):
    payloads, refs = refs[:members], refs[members:]
    own_logits_ref, alphas_ref, target_ref, small_ref = refs
    mine = lax.axis_index("member")
    block, classes = alphas_ref.shape
    target = jnp.zeros((block, classes), F32)
    logits = own_logits_ref[...]
    lse_total = jnp.zeros((1, LANES), F32)
    small_ref[...] = jnp.zeros_like(small_ref)
    for k in range(members):
        got = payloads[k]
        target += got[0:block, :].astype(F32)
        if k > 0:
            logits += got[block : 2 * block, :].astype(F32)
        tail = got[2 * block :, 0:LANES].astype(F32)
        lse = tail[0:1, :] + tail[1:2, :] + tail[2:3, :]
        lse_total += lse
        small_ref[pl.ds(mixed(mine, k, members, sender), 1), :] = lse
    target = target * (1.0 / members)
    alphas = jnp.exp(logits)
    alphas_ref[...] = alphas
    target_ref[...] = target
    sums = to_lanes(jnp.sum(alphas, axis=1, keepdims=True), LANES)
    parts = to_lanes(
        jnp.sum(log_gamma(alphas, logits) - (alphas - 1.0) * target, axis=1, keepdims=True), LANES
    )
    small_ref[members : members + 1, :] = sums
    small_ref[members + 1 : members + 2, :] = parts - lse_total * (1.0 / members) * (
        sums - float(classes)
    )


def digamma_kernel(alphas_ref, target_ref, inner_ref):
    inner_ref[...] = di_gamma(alphas_ref[...]) - target_ref[...]


def joined(parts, members):
    top = functools.reduce(jnp.maximum, parts)
    logs = top + jnp.log(sum(jnp.exp(part - top) for part in parts))
    line = lax.broadcasted_iota(jnp.int32, top.shape, 0)
    return jnp.where(line < members, logs, sum(parts))


def combine_kernel(members, own_ref, other_ref, out_ref):
    out_ref[...] = joined([own_ref[...], other_ref[...]], members)


def signal_kernel(members, chips, images, classes, *refs):
    smalls, refs = refs[:chips], refs[chips:]
    own_ref, alphas_ref, inner_ref, signal_ref, held = refs
    chip = lax.axis_index("dp") // 2
    block = alphas_ref.shape[0]
    for k in range(chips):
        held[mixed(chip, k, chips, sender)] = smalls[k][...]
    everything = joined([held[k] for k in range(chips)], members)
    norm_total = jnp.sum(everything[0:members, :], axis=0, keepdims=True) * (1.0 / members)
    own = jnp.sum(own_ref[0:members, :], axis=0, keepdims=True) * (1.0 / members)
    used = lax.broadcasted_iota(jnp.int32, (1, LANES), 1) < block
    alpha_sum = jnp.where(used, everything[members : members + 1, :], 1.0)
    shift = to_column(di_gamma(alpha_sum) + own - norm_total, block)
    width = alphas_ref.shape[1]
    signal_ref[:, 0:width] = (alphas_ref[...] * (inner_ref[...] - shift)).astype(BF16)
    terms = (
        everything[members + 1 : members + 2, :]
        - log_gamma(alpha_sum, jnp.log(alpha_sum))
        + norm_total * (alpha_sum - float(classes))
    )
    loss = jnp.sum(jnp.where(used, terms, 0.0), axis=1, keepdims=True)
    signal_ref[:, width:] = packed3(loss, block, LANES)


def gradient_kernel(members, images, classes, *refs):
    signals, refs = refs[:members], refs[members:]
    columns_ref, loss_ref, grad_ref, bias_ref, held, losses = refs
    mine = lax.axis_index("member")
    block = images // members
    width = held.shape[1]
    for k in range(members):
        at = mixed(mine, k, members, sender)
        held[slot(at, block), :] = signals[k][:, 0:width]
        tail = signals[k][:, width:].astype(F32)
        losses[pl.ds(at, 1), :] = tail[0:1, :] + tail[1:2, :] + tail[2:3, :]
    signal = held[...]
    grad = lax.dot_general(
        columns_ref[...], signal, (((0,), (0,)), ((), ())), preferred_element_type=F32
    )
    grad_ref[...] = grad * (1.0 / images)
    bias_ref[...] = jnp.sum(signal.astype(F32), axis=0) * (1.0 / images)
    loss_ref[0, 0] = jnp.sum(losses[:, 0:1]) * (1.0 / (images * classes))


def call(kernel, out_shape, scratch=(), in_specs=None, out_specs=None, flops=0):
    extra = {}
    if flops:
        extra["cost_estimate"] = pl.CostEstimate(flops=flops, bytes_accessed=0, transcendentals=0)
    if in_specs is not None:
        extra["in_specs"] = in_specs
    if out_specs is not None:
        extra["out_specs"] = out_specs
    return pl.pallas_call(
        kernel,
        out_shape=out_shape,
        scratch_shapes=list(scratch),
        compiler_params=pltpu.CompilerParams(vmem_limit_bytes=48 * 1024 * 1024),
        **extra,
    )


def on_device(
    teacher_feats,
    teacher_gain,
    teacher_head,
    teacher_bias,
    student_feats,
    student_gain,
    student_head,
    student_bias,
):
    members, peers = lax.axis_size("member"), lax.axis_size("dp")
    chips = peers // 2
    shape = jax.ShapeDtypeStruct
    here, far = pl.BlockSpec(memory_space=pltpu.VMEM), pl.BlockSpec(memory_space=pltpu.HBM)
    feats = teacher_feats[0]
    rows, depth = feats.shape
    block = student_feats.shape[0]
    images = rows * peers
    width, classes = student_head.shape
    small_rows = -(-(members + 2) // 8) * 8

    first = call(first_kernel, shape((8, LANES), F32), flops=1 << 28)()
    students = call(
        student_kernel, shape((members // 2 * block, depth), BF16), flops=1 << 33
    )(*[send_split(student_feats, j) for j in range(members // 2)], student_gain[None], first)
    parts = [feats] + [send(feats, "dp", k, 2) for k in range(1, chips)]
    own = call(
        functools.partial(join_kernel, chips),
        shape((chips * rows + members // 2 * block, depth), BF16),
        flops=1 << 33,
    )(*parts, students)
    *payloads, own_logits, own_columns = call(
        functools.partial(logits_kernel, members, rows),
        [shape((2 * block + PAD, classes), BF16)] * members
        + [shape((block, classes), F32), shape((images, width), BF16)],
        [
            pltpu.VMEM((images, depth), BF16),
            pltpu.VMEM((images, depth), BF16),
            pltpu.VMEM((images, classes), BF16),
            pltpu.VMEM((images, LANES), F32),
            pltpu.VMEM((images, classes), F32),
            pltpu.VMEM((block, depth), BF16),
            pltpu.VMEM((1, depth), F32),
            pltpu.VMEM((1, depth), F32),
            pltpu.VMEM((depth, classes), BF16),
            pltpu.VMEM((width, classes), BF16),
            pltpu.VMEM((1, classes), F32),
            pltpu.VMEM((classes,), F32),
            pltpu.SemaphoreType.DMA((7,)),
        ],
        [here] * 2 + [far] * 7,
    )(
        own,
        swap_cores(own, "dp"),
        student_feats,
        student_gain[None],
        teacher_gain,
        teacher_head[0],
        student_head,
        teacher_bias,
        student_bias,
    )
    got = [payloads[0]] + [send(payloads[k], "member", k) for k in range(1, members)]
    alphas, target, own = call(
        functools.partial(alphas_kernel, members),
        [shape((block, classes), F32)] * 2 + [shape((small_rows, LANES), F32)],
    )(*got, own_logits)
    other = swap_cores(own, "dp")
    inner = call(digamma_kernel, shape((block, classes), F32))(alphas, target)
    small = call(functools.partial(combine_kernel, members), shape(own.shape, F32))(own, other)
    smalls = [small] + [send(small, "dp", k, 2) for k in range(1, chips)]
    signal = call(
        functools.partial(signal_kernel, members, chips, images, classes * peers),
        shape((block, classes + LANES), BF16),
        [pltpu.VMEM((chips, small_rows, LANES), F32)],
    )(*smalls, own, alphas, inner)
    signals = [signal] + [send(signal, "member", k) for k in range(1, members)]
    loss, head_grad, bias_grad = call(
        functools.partial(gradient_kernel, members, images, classes * peers),
        [shape((1, 1), F32), shape((width, classes), F32), shape((classes,), F32)],
        [pltpu.VMEM((images, classes), BF16), pltpu.VMEM((members, LANES), F32)],
        out_specs=[pl.BlockSpec(memory_space=pltpu.SMEM), here, here],
    )(*signals, own_columns)
    return (loss[0, 0], head_grad, bias_grad)


def solution(mesh):
    placed = (
        P("member", "dp", None),
        P("member", None),
        P("member", None, "dp"),
        P("member", "dp"),
        P("member", None),
        P(),
        P("member", "dp"),
        P("dp"),
    )
    return jax.shard_map(
        on_device,
        mesh=mesh,
        in_specs=placed,
        out_specs=(P(), P("member", "dp"), P("dp")),
        check_vma=False,
    )
```

```python
import functools
import math

import jax
import jax.numpy as jnp
from jax import lax
from jax.experimental import pallas as pl
from jax.experimental.pallas import tpu as pltpu
from jax.sharding import PartitionSpec as P

BF16, F32 = jnp.bfloat16, jnp.float32
LANES = 128
PAD = 16
LANCZOS = (
    0.99999999999980993227684700473478,
    676.520368121885098567009190444019,
    -1259.13921672240287047156078755283,
    771.3234287776530788486528258894,
    -176.61502916214059906584551354,
    12.507343278686904814458936853,
    -0.13857109526572011689554707,
    9.984369578019570859563e-6,
    1.50563273514931155834e-7,
)


def partner(index, k, size):
    return index ^ k if size & (size - 1) == 0 else (index + k) % size


def sender(index, k, size):
    return index ^ k if size & (size - 1) == 0 else (index - k + size) % size


def mixed(index, k, size, of):
    if size & (size - 1) == 0:
        return lax.bitwise_xor(index, jnp.int32(k) if isinstance(k, int) else k)
    step = k if of is partner else size - k
    return lax.rem(index + step, jnp.int32(size))


def send(value, axis, k, scale=1, groups=1):
    size = lax.axis_size(axis) // scale
    pairs = [
        (outer * scale + inner, partner(outer, k, size) * scale + inner)
        for outer in range(size)
        for inner in range(scale)
    ]
    return lax.ppermute(value, axis, pairs)


def split_step(j, core, members):
    return jnp.where(core == 0, 2 * j + 1, 2 * j + 2 if 2 * j + 2 < members else 1)


def send_split(value, j):
    members, peers = lax.axis_size("member"), lax.axis_size("dp")
    steps = 2 * j + 1, (2 * j + 2 if 2 * j + 2 < members else 1)
    pairs = [
        (m * peers + d, partner(m, steps[d % 2], members) * peers + d)
        for m in range(members)
        for d in range(peers)
    ]
    return lax.ppermute(value, ("member", "dp"), pairs)


def swap_cores(value, axis):
    return lax.ppermute(value, axis, [(i, i ^ 1) for i in range(lax.axis_size(axis))])


def normed(values, gain_row):
    values = values.astype(F32)
    center = values - jnp.mean(values, axis=-1, keepdims=True)
    spread = jnp.mean(center * center, axis=-1, keepdims=True)
    return (center * lax.rsqrt(spread + 1e-06) * gain_row).astype(BF16)


def split3(value):
    high = value.astype(BF16)
    rest = value - high.astype(F32)
    middle = rest.astype(BF16)
    return high, middle, (rest - middle.astype(F32)).astype(BF16)


def diagonal(rows, lanes):
    return lax.broadcasted_iota(jnp.int32, (rows, lanes), 0) == lax.broadcasted_iota(
        jnp.int32, (rows, lanes), 1
    )


def to_lanes(column, lanes):
    return jnp.sum(
        jnp.where(diagonal(column.shape[0], lanes), column, 0.0), axis=0, keepdims=True
    )


def to_column(row, rows):
    return jnp.sum(jnp.where(diagonal(rows, row.shape[1]), row, 0.0), axis=1, keepdims=True)


def series(x):
    total = jnp.full_like(x, LANCZOS[0])
    slope = jnp.zeros_like(x)
    for k in range(1, 9):
        inverse = 1.0 / (x + float(k))
        term = LANCZOS[k] * inverse
        total = total + term
        slope = slope - term * inverse
    log_t = math.log(7.5) + jnp.log1p(x / 7.5)
    return total, slope, log_t


def log_gamma(x, log_x):
    total, _, log_t = series(x)
    t = x + 7.5
    return (
        (x + 0.5 - t / log_t) * log_t
        + 0.5 * math.log(2.0 * math.pi)
        + jnp.log(total)
        - log_x
    )


def di_gamma(x):
    total, slope, log_t = series(x)
    return log_t + slope / total - 7.0 / (x + 7.5) - 1.0 / x


def slot(at, rows):
    return pl.ds(pl.multiple_of(at * rows, rows), rows)


def first_kernel(out_ref):
    out_ref[...] = jnp.zeros_like(out_ref)


def student_kernel(*refs):
    *parts, gain_ref, _, out_ref = refs
    rows = parts[0].shape[0]
    for j, part in enumerate(parts):
        out_ref[j * rows : (j + 1) * rows, :] = normed(part[...], gain_ref[...])


def join_kernel(chips, *refs):
    *parts, gain_ref, student_ref, out_ref = refs
    chip = lax.axis_index("dp") // 2
    rows = parts[0].shape[0]
    for k in range(chips):
        out_ref[slot(mixed(chip, k, chips, sender), rows), :] = normed(parts[k][...], gain_ref[...])
    start = chips * rows
    out_ref[start:, :] = student_ref[...]


def packed3(row, rows, lanes):
    line = lax.broadcasted_iota(jnp.int32, (rows, lanes), 0)
    high, middle, low = (part.astype(F32) for part in split3(row))
    lower = jnp.where(line == 2, low, 0.0)
    return jnp.where(line == 0, high, jnp.where(line == 1, middle, lower)).astype(BF16)


def logits_kernel(members, rows, *refs):
    own_ref, other_ref, refs = refs[0], refs[1], refs[2:]
    feats_ref, student_gain_ref, head_ref, student_ref, bias_ref, student_bias_ref = refs[:6]
    refs = refs[6:]
    payloads, refs = refs[:members], refs[members:]
    own_logits_ref, columns_ref, gathered, held, shifted_ref, lse_ref, partial_ref = refs
    mine, place = lax.axis_index("member"), lax.axis_index("dp")
    core = lax.rem(place, jnp.int32(2))
    chips = gathered.shape[0] // (2 * rows)
    block = feats_ref.shape[0]
    width = columns_ref.shape[1]
    held[slot(mine, block), :] = normed(feats_ref[...], student_gain_ref[...])
    for source, side in ((own_ref, core), (other_ref, 1 - core)):
        for chip in range(chips):
            at = slot(2 * chip + side, rows)
            gathered[at, :] = source[chip * rows : (chip + 1) * rows, :]
        for j in range(members // 2):
            start = chips * rows + j * block
            at = slot(mixed(mine, split_step(j, side, members), members, sender), block)
            held[at, :] = source[start : start + block, :]
    if width % LANES == 0:
        columns_ref[...] = held[:, pl.ds(pl.multiple_of(mine * width, LANES), width)]
    else:
        for j in range(members):

            @pl.when(mine == j)
            def _(j=j):
                columns_ref[...] = held[:, j * width : (j + 1) * width]

    logits = jnp.dot(gathered[...], head_ref[...], preferred_element_type=F32) + bias_ref[...]
    top = jnp.max(logits, axis=1, keepdims=True)
    lse = top + jnp.log(jnp.sum(jnp.exp(logits - top), axis=1, keepdims=True))
    shifted_ref[...] = (logits - lse).astype(BF16)
    lse_ref[...] = jnp.broadcast_to(lse, lse_ref.shape)
    partial_ref[...] = jnp.dot(columns_ref[...], student_ref[...], preferred_element_type=F32)
    classes = logits.shape[1]
    for k in range(members):
        at = slot(mixed(mine, k, members, partner), block)
        out = payloads[k]
        out[0:block, :] = shifted_ref[at, :]
        if k == 0:
            own_logits_ref[...] = partial_ref[at, :] + student_bias_ref[...][None, :]
        out[block : 2 * block, :] = partial_ref[at, :].astype(BF16)
        out[2 * block :, :] = packed3(to_lanes(lse_ref[at, 0:1], classes), PAD, classes)


def alphas_kernel(members, *refs):
    payloads, refs = refs[:members], refs[members:]
    own_logits_ref, alphas_ref, target_ref, small_ref = refs
    mine = lax.axis_index("member")
    block, classes = alphas_ref.shape
    target = jnp.zeros((block, classes), F32)
    logits = own_logits_ref[...]
    lse_total = jnp.zeros((1, LANES), F32)
    small_ref[...] = jnp.zeros_like(small_ref)
    for k in range(members):
        got = payloads[k]
        target += got[0:block, :].astype(F32)
        if k > 0:
            logits += got[block : 2 * block, :].astype(F32)
        tail = got[2 * block :, 0:LANES].astype(F32)
        lse = tail[0:1, :] + tail[1:2, :] + tail[2:3, :]
        lse_total += lse
        small_ref[pl.ds(mixed(mine, k, members, sender), 1), :] = lse
    target = target * (1.0 / members)
    alphas = jnp.exp(logits)
    alphas_ref[...] = alphas
    target_ref[...] = target
    sums = to_lanes(jnp.sum(alphas, axis=1, keepdims=True), LANES)
    parts = to_lanes(
        jnp.sum(log_gamma(alphas, logits) - (alphas - 1.0) * target, axis=1, keepdims=True), LANES
    )
    small_ref[members : members + 1, :] = sums
    small_ref[members + 1 : members + 2, :] = parts - lse_total * (1.0 / members) * (
        sums - float(classes)
    )


def digamma_kernel(alphas_ref, target_ref, columns_ref, inner_ref, turned_ref):
    turned_ref[...] = columns_ref[...].T
    inner_ref[...] = di_gamma(alphas_ref[...]) - target_ref[...]


def joined(parts, members):
    top = functools.reduce(jnp.maximum, parts)
    logs = top + jnp.log(sum(jnp.exp(part - top) for part in parts))
    line = lax.broadcasted_iota(jnp.int32, top.shape, 0)
    return jnp.where(line < members, logs, sum(parts))


def combine_kernel(members, own_ref, other_ref, out_ref):
    out_ref[...] = joined([own_ref[...], other_ref[...]], members)


def signal_kernel(members, chips, images, classes, *refs):
    smalls, refs = refs[:chips], refs[chips:]
    own_ref, alphas_ref, inner_ref, signal_ref, held = refs
    chip = lax.axis_index("dp") // 2
    block = alphas_ref.shape[0]
    for k in range(chips):
        held[mixed(chip, k, chips, sender)] = smalls[k][...]
    everything = joined([held[k] for k in range(chips)], members)
    norm_total = jnp.sum(everything[0:members, :], axis=0, keepdims=True) * (1.0 / members)
    own = jnp.sum(own_ref[0:members, :], axis=0, keepdims=True) * (1.0 / members)
    used = lax.broadcasted_iota(jnp.int32, (1, LANES), 1) < block
    alpha_sum = jnp.where(used, everything[members : members + 1, :], 1.0)
    shift = to_column(di_gamma(alpha_sum) + own - norm_total, block)
    width = alphas_ref.shape[1]
    signal_ref[:, 0:width] = (alphas_ref[...] * (inner_ref[...] - shift)).astype(BF16)
    terms = (
        everything[members + 1 : members + 2, :]
        - log_gamma(alpha_sum, jnp.log(alpha_sum))
        + norm_total * (alpha_sum - float(classes))
    )
    loss = jnp.sum(jnp.where(used, terms, 0.0), axis=1, keepdims=True)
    signal_ref[:, width:] = packed3(loss, block, LANES)


def gradient_kernel(members, images, classes, *refs):
    signals, refs = refs[:members], refs[members:]
    turned_ref, loss_ref, grad_ref, bias_ref, held, losses = refs
    mine = lax.axis_index("member")
    block = images // members
    width = held.shape[1]
    for k in range(members):
        at = mixed(mine, k, members, sender)
        held[slot(at, block), :] = signals[k][:, 0:width]
        tail = signals[k][:, width:].astype(F32)
        losses[pl.ds(at, 1), :] = tail[0:1, :] + tail[1:2, :] + tail[2:3, :]
    signal = held[...]
    grad = jnp.dot(turned_ref[...], signal, preferred_element_type=F32)
    grad_ref[...] = grad * (1.0 / images)
    bias_ref[...] = jnp.sum(signal.astype(F32), axis=0) * (1.0 / images)
    loss_ref[0, 0] = jnp.sum(losses[:, 0:1]) * (1.0 / (images * classes))


def call(kernel, out_shape, scratch=(), out_specs=None, flops=0):
    extra = {}
    if flops:
        extra["cost_estimate"] = pl.CostEstimate(flops=flops, bytes_accessed=0, transcendentals=0)
    if out_specs is not None:
        extra["out_specs"] = out_specs
    return pl.pallas_call(
        kernel,
        out_shape=out_shape,
        scratch_shapes=list(scratch),
        compiler_params=pltpu.CompilerParams(vmem_limit_bytes=48 * 1024 * 1024),
        **extra,
    )


def on_device(
    teacher_feats,
    teacher_gain,
    teacher_head,
    teacher_bias,
    student_feats,
    student_gain,
    student_head,
    student_bias,
):
    members, peers = lax.axis_size("member"), lax.axis_size("dp")
    chips = peers // 2
    shape = jax.ShapeDtypeStruct
    here = pl.BlockSpec(memory_space=pltpu.VMEM)
    feats = teacher_feats[0]
    rows, depth = feats.shape
    block = student_feats.shape[0]
    images = rows * peers
    width, classes = student_head.shape
    small_rows = -(-(members + 2) // 8) * 8

    first = call(first_kernel, shape((8, LANES), F32), flops=1 << 28)()
    students = call(
        student_kernel, shape((members // 2 * block, depth), BF16), flops=1 << 33
    )(*[send_split(student_feats, j) for j in range(members // 2)], student_gain[None], first)
    parts = [feats] + [send(feats, "dp", k, 2) for k in range(1, chips)]
    own = call(
        functools.partial(join_kernel, chips),
        shape((chips * rows + members // 2 * block, depth), BF16),
        flops=1 << 33,
    )(*parts, teacher_gain, students)
    *payloads, own_logits, own_columns = call(
        functools.partial(logits_kernel, members, rows),
        [shape((2 * block + PAD, classes), BF16)] * members
        + [shape((block, classes), F32), shape((images, width), BF16)],
        [
            pltpu.VMEM((images, depth), BF16),
            pltpu.VMEM((images, depth), BF16),
            pltpu.VMEM((images, classes), BF16),
            pltpu.VMEM((images, LANES), F32),
            pltpu.VMEM((images, classes), F32),
        ],
    )(
        own,
        swap_cores(own, "dp"),
        student_feats,
        student_gain[None],
        teacher_head[0],
        student_head,
        teacher_bias,
        student_bias,
    )
    got = [payloads[0]] + [send(payloads[k], "member", k) for k in range(1, members)]
    alphas, target, own = call(
        functools.partial(alphas_kernel, members),
        [shape((block, classes), F32)] * 2 + [shape((small_rows, LANES), F32)],
    )(*got, own_logits)
    other = swap_cores(own, "dp")
    inner, turned = call(
        digamma_kernel, [shape((block, classes), F32), shape((width, images), BF16)]
    )(alphas, target, own_columns)
    small = call(functools.partial(combine_kernel, members), shape(own.shape, F32))(own, other)
    smalls = [small] + [send(small, "dp", k, 2) for k in range(1, chips)]
    signal = call(
        functools.partial(signal_kernel, members, chips, images, classes * peers),
        shape((block, classes + LANES), BF16),
        [pltpu.VMEM((chips, small_rows, LANES), F32)],
    )(*smalls, own, alphas, inner)
    signals = [signal] + [send(signal, "member", k) for k in range(1, members)]
    loss, head_grad, bias_grad = call(
        functools.partial(gradient_kernel, members, images, classes * peers),
        [shape((1, 1), F32), shape((width, classes), F32), shape((classes,), F32)],
        [pltpu.VMEM((images, classes), BF16), pltpu.VMEM((members, LANES), F32)],
        out_specs=[pl.BlockSpec(memory_space=pltpu.SMEM), here, here],
    )(*signals, turned)
    return (loss[0, 0], head_grad, bias_grad)


def solution(mesh):
    placed = (
        P("member", "dp", None),
        P("member", None),
        P("member", None, "dp"),
        P("member", "dp"),
        P("member", None),
        P(),
        P("member", "dp"),
        P("dp"),
    )
    return jax.shard_map(
        on_device,
        mesh=mesh,
        in_specs=placed,
        out_specs=(P(), P("member", "dp"), P("dp")),
        check_vma=False,
    )
```

```python
import functools
import math

import jax
import jax.numpy as jnp
from jax import lax
from jax.experimental import pallas as pl
from jax.experimental.pallas import tpu as pltpu
from jax.sharding import PartitionSpec as P

BF16, F32 = jnp.bfloat16, jnp.float32
LANES = 128
PAD = 8
LANCZOS = (
    0.99999999999980993227684700473478,
    676.520368121885098567009190444019,
    -1259.13921672240287047156078755283,
    771.3234287776530788486528258894,
    -176.61502916214059906584551354,
    12.507343278686904814458936853,
    -0.13857109526572011689554707,
    9.984369578019570859563e-6,
    1.50563273514931155834e-7,
)


def partner(index, k, size):
    return index ^ k if size & (size - 1) == 0 else (index + k) % size


def sender(index, k, size):
    return index ^ k if size & (size - 1) == 0 else (index - k + size) % size


def mixed(index, k, size, of):
    if size & (size - 1) == 0:
        return lax.bitwise_xor(index, jnp.int32(k) if isinstance(k, int) else k)
    step = k if of is partner else size - k
    return lax.rem(index + step, jnp.int32(size))


def send(value, axis, k, scale=1, groups=1):
    size = lax.axis_size(axis) // scale
    pairs = [
        (outer * scale + inner, partner(outer, k, size) * scale + inner)
        for outer in range(size)
        for inner in range(scale)
    ]
    return lax.ppermute(value, axis, pairs)


def split_step(j, core, members):
    return jnp.where(core == 0, 2 * j + 1, 2 * j + 2 if 2 * j + 2 < members else 1)


def send_split(value, j):
    members, peers = lax.axis_size("member"), lax.axis_size("dp")
    steps = 2 * j + 1, (2 * j + 2 if 2 * j + 2 < members else 1)
    pairs = [
        (m * peers + d, partner(m, steps[d % 2], members) * peers + d)
        for m in range(members)
        for d in range(peers)
    ]
    return lax.ppermute(value, ("member", "dp"), pairs)


def swap_cores(value, axis):
    return lax.ppermute(value, axis, [(i, i ^ 1) for i in range(lax.axis_size(axis))])


def normed(values, gain_row):
    values = values.astype(F32)
    center = values - jnp.mean(values, axis=-1, keepdims=True)
    spread = jnp.mean(center * center, axis=-1, keepdims=True)
    return (center * lax.rsqrt(spread + 1e-06) * gain_row).astype(BF16)


def split3(value):
    high = value.astype(BF16)
    rest = value - high.astype(F32)
    middle = rest.astype(BF16)
    return high, middle, (rest - middle.astype(F32)).astype(BF16)


def diagonal(rows, lanes):
    return lax.broadcasted_iota(jnp.int32, (rows, lanes), 0) == lax.broadcasted_iota(
        jnp.int32, (rows, lanes), 1
    )


def to_lanes(column, lanes):
    return jnp.sum(
        jnp.where(diagonal(column.shape[0], lanes), column, 0.0), axis=0, keepdims=True
    )


def to_column(row, rows):
    return jnp.sum(jnp.where(diagonal(rows, row.shape[1]), row, 0.0), axis=1, keepdims=True)


def series(x):
    total = jnp.full_like(x, LANCZOS[0])
    slope = jnp.zeros_like(x)
    for k in range(1, 9):
        inverse = 1.0 / (x + float(k))
        term = LANCZOS[k] * inverse
        total = total + term
        slope = slope - term * inverse
    log_t = math.log(7.5) + jnp.log1p(x / 7.5)
    return total, slope, log_t


def log_gamma(x, log_x):
    total, _, log_t = series(x)
    t = x + 7.5
    return (
        (x + 0.5 - t / log_t) * log_t
        + 0.5 * math.log(2.0 * math.pi)
        + jnp.log(total)
        - log_x
    )


def di_gamma(x):
    total, slope, log_t = series(x)
    return log_t + slope / total - 7.0 / (x + 7.5) - 1.0 / x


def slot(at, rows):
    return pl.ds(pl.multiple_of(at * rows, rows), rows)


def first_kernel(out_ref):
    out_ref[...] = jnp.zeros_like(out_ref)


def student_kernel(*refs):
    *parts, gain_ref, _, out_ref = refs
    rows = parts[0].shape[0]
    for j, part in enumerate(parts):
        out_ref[j * rows : (j + 1) * rows, :] = normed(part[...], gain_ref[...])


def join_kernel(chips, *refs):
    *parts, gain_ref, student_ref, out_ref = refs
    chip = lax.axis_index("dp") // 2
    rows = parts[0].shape[0]
    for k in range(chips):
        out_ref[slot(mixed(chip, k, chips, sender), rows), :] = normed(parts[k][...], gain_ref[...])
    start = chips * rows
    out_ref[start:, :] = student_ref[...]


def packed3(row, rows, lanes):
    line = lax.broadcasted_iota(jnp.int32, (rows, lanes), 0)
    high, middle, low = (part.astype(F32) for part in split3(row))
    lower = jnp.where(line == 2, low, 0.0)
    return jnp.where(line == 0, high, jnp.where(line == 1, middle, lower)).astype(BF16)


def logits_kernel(members, rows, *refs):
    own_ref, other_ref, refs = refs[0], refs[1], refs[2:]
    feats_ref, student_gain_ref, head_ref, student_ref, bias_ref, student_bias_ref = refs[:6]
    refs = refs[6:]
    payloads, refs = refs[:members], refs[members:]
    own_logits_ref, columns_ref, gathered, held, shifted_ref, lse_ref, partial_ref = refs
    mine, place = lax.axis_index("member"), lax.axis_index("dp")
    core = lax.rem(place, jnp.int32(2))
    chips = gathered.shape[0] // (2 * rows)
    block = feats_ref.shape[0]
    width = columns_ref.shape[1]
    held[slot(mine, block), :] = normed(feats_ref[...], student_gain_ref[...])
    for source, side in ((own_ref, core), (other_ref, 1 - core)):
        for chip in range(chips):
            at = slot(2 * chip + side, rows)
            gathered[at, :] = source[chip * rows : (chip + 1) * rows, :]
        for j in range(members // 2):
            start = chips * rows + j * block
            at = slot(mixed(mine, split_step(j, side, members), members, sender), block)
            held[at, :] = source[start : start + block, :]
    if width % LANES == 0:
        columns_ref[...] = held[:, pl.ds(pl.multiple_of(mine * width, LANES), width)]
    else:
        for j in range(members):

            @pl.when(mine == j)
            def _(j=j):
                columns_ref[...] = held[:, j * width : (j + 1) * width]

    logits = jnp.dot(gathered[...], head_ref[...], preferred_element_type=F32) + bias_ref[...]
    top = jnp.max(logits, axis=1, keepdims=True)
    lse = top + jnp.log(jnp.sum(jnp.exp(logits - top), axis=1, keepdims=True))
    shifted_ref[...] = (logits - lse).astype(BF16)
    lse_ref[...] = jnp.broadcast_to(lse, lse_ref.shape)
    partial_ref[...] = jnp.dot(columns_ref[...], student_ref[...], preferred_element_type=F32)
    classes = logits.shape[1]
    for k in range(members):
        at = slot(mixed(mine, k, members, partner), block)
        out = payloads[k]
        out[0:block, :] = shifted_ref[at, :]
        if k == 0:
            own_logits_ref[...] = partial_ref[at, :] + student_bias_ref[...][None, :]
        out[block : 2 * block, :] = partial_ref[at, :].astype(BF16)
        out[2 * block :, :] = packed3(to_lanes(lse_ref[at, 0:1], classes), PAD, classes)


def alphas_kernel(members, *refs):
    payloads, refs = refs[:members], refs[members:]
    own_logits_ref, alphas_ref, target_ref, small_ref = refs
    mine = lax.axis_index("member")
    block, classes = alphas_ref.shape
    target = jnp.zeros((block, classes), F32)
    logits = own_logits_ref[...]
    lse_total = jnp.zeros((1, LANES), F32)
    small_ref[...] = jnp.zeros_like(small_ref)
    for k in range(members):
        got = payloads[k]
        target += got[0:block, :].astype(F32)
        if k > 0:
            logits += got[block : 2 * block, :].astype(F32)
        tail = got[2 * block :, 0:LANES].astype(F32)
        lse = tail[0:1, :] + tail[1:2, :] + tail[2:3, :]
        lse_total += lse
        small_ref[pl.ds(mixed(mine, k, members, sender), 1), :] = lse
    target = target * (1.0 / members)
    alphas = jnp.exp(logits)
    alphas_ref[...] = alphas
    target_ref[...] = target
    sums = to_lanes(jnp.sum(alphas, axis=1, keepdims=True), LANES)
    parts = to_lanes(
        jnp.sum(log_gamma(alphas, logits) - (alphas - 1.0) * target, axis=1, keepdims=True), LANES
    )
    small_ref[members : members + 1, :] = sums
    small_ref[members + 1 : members + 2, :] = parts - lse_total * (1.0 / members) * (
        sums - float(classes)
    )


def digamma_kernel(alphas_ref, target_ref, columns_ref, inner_ref, turned_ref):
    turned_ref[...] = columns_ref[...].T
    inner_ref[...] = di_gamma(alphas_ref[...]) - target_ref[...]


def joined(parts, members):
    top = functools.reduce(jnp.maximum, parts)
    logs = top + jnp.log(sum(jnp.exp(part - top) for part in parts))
    line = lax.broadcasted_iota(jnp.int32, top.shape, 0)
    return jnp.where(line < members, logs, sum(parts))


def combine_kernel(members, own_ref, other_ref, out_ref):
    out_ref[...] = joined([own_ref[...], other_ref[...]], members)


def signal_kernel(members, chips, images, classes, *refs):
    smalls, refs = refs[:chips], refs[chips:]
    own_ref, alphas_ref, inner_ref, signal_ref, held = refs
    chip = lax.axis_index("dp") // 2
    block = alphas_ref.shape[0]
    for k in range(chips):
        held[mixed(chip, k, chips, sender)] = smalls[k][...]
    everything = joined([held[k] for k in range(chips)], members)
    norm_total = jnp.sum(everything[0:members, :], axis=0, keepdims=True) * (1.0 / members)
    own = jnp.sum(own_ref[0:members, :], axis=0, keepdims=True) * (1.0 / members)
    used = lax.broadcasted_iota(jnp.int32, (1, LANES), 1) < block
    alpha_sum = jnp.where(used, everything[members : members + 1, :], 1.0)
    shift = to_column(di_gamma(alpha_sum) + own - norm_total, block)
    width = alphas_ref.shape[1]
    signal_ref[:, 0:width] = (alphas_ref[...] * (inner_ref[...] - shift)).astype(BF16)
    terms = (
        everything[members + 1 : members + 2, :]
        - log_gamma(alpha_sum, jnp.log(alpha_sum))
        + norm_total * (alpha_sum - float(classes))
    )
    loss = jnp.sum(jnp.where(used, terms, 0.0), axis=1, keepdims=True)
    signal_ref[:, width:] = packed3(loss, block, LANES)


def gradient_kernel(members, images, classes, *refs):
    signals, refs = refs[:members], refs[members:]
    turned_ref, loss_ref, grad_ref, bias_ref, held, losses = refs
    mine = lax.axis_index("member")
    block = images // members
    width = held.shape[1]
    for k in range(members):
        at = mixed(mine, k, members, sender)
        held[slot(at, block), :] = signals[k][:, 0:width]
        tail = signals[k][:, width:].astype(F32)
        losses[pl.ds(at, 1), :] = tail[0:1, :] + tail[1:2, :] + tail[2:3, :]
    signal = held[...]
    grad = jnp.dot(turned_ref[...], signal, preferred_element_type=F32)
    grad_ref[...] = grad * (1.0 / images)
    bias_ref[...] = jnp.sum(signal.astype(F32), axis=0) * (1.0 / images)
    loss_ref[0, 0] = jnp.sum(losses[:, 0:1]) * (1.0 / (images * classes))


def call(kernel, out_shape, scratch=(), out_specs=None, flops=0):
    extra = {}
    if flops:
        extra["cost_estimate"] = pl.CostEstimate(flops=flops, bytes_accessed=0, transcendentals=0)
    if out_specs is not None:
        extra["out_specs"] = out_specs
    return pl.pallas_call(
        kernel,
        out_shape=out_shape,
        scratch_shapes=list(scratch),
        compiler_params=pltpu.CompilerParams(vmem_limit_bytes=48 * 1024 * 1024),
        **extra,
    )


def on_device(
    teacher_feats,
    teacher_gain,
    teacher_head,
    teacher_bias,
    student_feats,
    student_gain,
    student_head,
    student_bias,
):
    members, peers = lax.axis_size("member"), lax.axis_size("dp")
    chips = peers // 2
    shape = jax.ShapeDtypeStruct
    here = pl.BlockSpec(memory_space=pltpu.VMEM)
    feats = teacher_feats[0]
    rows, depth = feats.shape
    block = student_feats.shape[0]
    images = rows * peers
    width, classes = student_head.shape
    small_rows = -(-(members + 2) // 8) * 8

    first = call(first_kernel, shape((8, LANES), F32), flops=1 << 28)()
    students = call(
        student_kernel, shape((members // 2 * block, depth), BF16), flops=1 << 33
    )(*[send_split(student_feats, j) for j in range(members // 2)], student_gain[None], first)
    parts = [feats] + [send(feats, "dp", k, 2) for k in range(1, chips)]
    own = call(
        functools.partial(join_kernel, chips),
        shape((chips * rows + members // 2 * block, depth), BF16),
        flops=1 << 33,
    )(*parts, teacher_gain, students)
    *payloads, own_logits, own_columns = call(
        functools.partial(logits_kernel, members, rows),
        [shape((2 * block + PAD, classes), BF16)] * members
        + [shape((block, classes), F32), shape((images, width), BF16)],
        [
            pltpu.VMEM((images, depth), BF16),
            pltpu.VMEM((images, depth), BF16),
            pltpu.VMEM((images, classes), BF16),
            pltpu.VMEM((images, LANES), F32),
            pltpu.VMEM((images, classes), F32),
        ],
    )(
        own,
        swap_cores(own, "dp"),
        student_feats,
        student_gain[None],
        teacher_head[0],
        student_head,
        teacher_bias,
        student_bias,
    )
    got = [payloads[0]] + [send(payloads[k], "member", k) for k in range(1, members)]
    alphas, target, own = call(
        functools.partial(alphas_kernel, members),
        [shape((block, classes), F32)] * 2 + [shape((small_rows, LANES), F32)],
    )(*got, own_logits)
    other = swap_cores(own, "dp")
    inner, turned = call(
        digamma_kernel, [shape((block, classes), F32), shape((width, images), BF16)]
    )(alphas, target, own_columns)
    small = call(functools.partial(combine_kernel, members), shape(own.shape, F32))(own, other)
    smalls = [small] + [send(small, "dp", k, 2) for k in range(1, chips)]
    signal = call(
        functools.partial(signal_kernel, members, chips, images, classes * peers),
        shape((block, classes + LANES), BF16),
        [pltpu.VMEM((chips, small_rows, LANES), F32)],
    )(*smalls, own, alphas, inner)
    signals = [signal] + [send(signal, "member", k) for k in range(1, members)]
    loss, head_grad, bias_grad = call(
        functools.partial(gradient_kernel, members, images, classes * peers),
        [shape((1, 1), F32), shape((width, classes), F32), shape((classes,), F32)],
        [pltpu.VMEM((images, classes), BF16), pltpu.VMEM((members, LANES), F32)],
        out_specs=[pl.BlockSpec(memory_space=pltpu.SMEM), here, here],
    )(*signals, turned)
    return (loss[0, 0], head_grad, bias_grad)


def solution(mesh):
    placed = (
        P("member", "dp", None),
        P("member", None),
        P("member", None, "dp"),
        P("member", "dp"),
        P("member", None),
        P(),
        P("member", "dp"),
        P("dp"),
    )
    return jax.shard_map(
        on_device,
        mesh=mesh,
        in_specs=placed,
        out_specs=(P(), P("member", "dp"), P("dp")),
        check_vma=False,
    )
```

```python
import functools
import math

import jax
import jax.numpy as jnp
from jax import lax
from jax.experimental import pallas as pl
from jax.experimental.pallas import tpu as pltpu
from jax.sharding import PartitionSpec as P

BF16, F32 = jnp.bfloat16, jnp.float32
LANES = 128
PAD = 8
LANCZOS = (
    0.99999999999980993227684700473478,
    676.520368121885098567009190444019,
    -1259.13921672240287047156078755283,
    771.3234287776530788486528258894,
    -176.61502916214059906584551354,
    12.507343278686904814458936853,
    -0.13857109526572011689554707,
    9.984369578019570859563e-6,
    1.50563273514931155834e-7,
)


def partner(index, k, size):
    return index ^ k if size & (size - 1) == 0 else (index + k) % size


def sender(index, k, size):
    return index ^ k if size & (size - 1) == 0 else (index - k + size) % size


def mixed(index, k, size, of):
    if size & (size - 1) == 0:
        return lax.bitwise_xor(index, jnp.int32(k) if isinstance(k, int) else k)
    step = k if of is partner else size - k
    return lax.rem(index + step, jnp.int32(size))


def send(value, axis, k, scale=1, groups=1):
    size = lax.axis_size(axis) // scale
    pairs = [
        (outer * scale + inner, partner(outer, k, size) * scale + inner)
        for outer in range(size)
        for inner in range(scale)
    ]
    return lax.ppermute(value, axis, pairs)


def split_step(j, core, members):
    return jnp.where(core == 0, 2 * j + 1, 2 * j + 2 if 2 * j + 2 < members else 1)


def send_split(value, j):
    members, peers = lax.axis_size("member"), lax.axis_size("dp")
    steps = 2 * j + 1, (2 * j + 2 if 2 * j + 2 < members else 1)
    pairs = [
        (m * peers + d, partner(m, steps[d % 2], members) * peers + d)
        for m in range(members)
        for d in range(peers)
    ]
    return lax.ppermute(value, ("member", "dp"), pairs)


def swap_cores(value, axis):
    return lax.ppermute(value, axis, [(i, i ^ 1) for i in range(lax.axis_size(axis))])


def normed(values, gain_row):
    values = values.astype(F32)
    center = values - jnp.mean(values, axis=-1, keepdims=True)
    spread = jnp.mean(center * center, axis=-1, keepdims=True)
    return (center * lax.rsqrt(spread + 1e-06) * gain_row).astype(BF16)


def split3(value):
    high = value.astype(BF16)
    rest = value - high.astype(F32)
    middle = rest.astype(BF16)
    return high, middle, (rest - middle.astype(F32)).astype(BF16)


def diagonal(rows, lanes):
    return lax.broadcasted_iota(jnp.int32, (rows, lanes), 0) == lax.broadcasted_iota(
        jnp.int32, (rows, lanes), 1
    )


def to_lanes(column, lanes):
    return jnp.sum(
        jnp.where(diagonal(column.shape[0], lanes), column, 0.0), axis=0, keepdims=True
    )


def to_column(row, rows):
    return jnp.sum(jnp.where(diagonal(rows, row.shape[1]), row, 0.0), axis=1, keepdims=True)


def series(x):
    total = jnp.full_like(x, LANCZOS[0])
    slope = jnp.zeros_like(x)
    for k in range(1, 9):
        inverse = 1.0 / (x + float(k))
        term = LANCZOS[k] * inverse
        total = total + term
        slope = slope - term * inverse
    log_t = math.log(7.5) + jnp.log1p(x / 7.5)
    return total, slope, log_t


def log_gamma(x, log_x):
    total, _, log_t = series(x)
    t = x + 7.5
    return (
        (x + 0.5 - t / log_t) * log_t
        + 0.5 * math.log(2.0 * math.pi)
        + jnp.log(total)
        - log_x
    )


def di_gamma(x):
    total, slope, log_t = series(x)
    return log_t + slope / total - 7.0 / (x + 7.5) - 1.0 / x


def slot(at, rows):
    return pl.ds(pl.multiple_of(at * rows, rows), rows)


def first_kernel(out_ref):
    out_ref[...] = jnp.zeros_like(out_ref)


def student_kernel(*refs):
    *parts, gain_ref, _, out_ref = refs
    rows = parts[0].shape[0]
    for j, part in enumerate(parts):
        out_ref[j * rows : (j + 1) * rows, :] = normed(part[...], gain_ref[...])


def join_kernel(chips, *refs):
    *parts, gain_ref, student_ref, out_ref = refs
    chip = lax.axis_index("dp") // 2
    rows = parts[0].shape[0]
    for k in range(chips):
        out_ref[slot(mixed(chip, k, chips, sender), rows), :] = normed(parts[k][...], gain_ref[...])
    start = chips * rows
    out_ref[start:, :] = student_ref[...]


def packed3(row, rows, lanes):
    line = lax.broadcasted_iota(jnp.int32, (rows, lanes), 0)
    high, middle, low = (part.astype(F32) for part in split3(row))
    lower = jnp.where(line == 2, low, 0.0)
    return jnp.where(line == 0, high, jnp.where(line == 1, middle, lower)).astype(BF16)


def logits_kernel(members, rows, *refs):
    own_ref, other_ref, refs = refs[0], refs[1], refs[2:]
    feats_ref, student_gain_ref, head_ref, student_ref, bias_ref, student_bias_ref = refs[:6]
    refs = refs[6:]
    payloads, refs = refs[:members], refs[members:]
    own_logits_ref, columns_ref, gathered, held, shifted_ref, lse_ref, partial_ref = refs
    mine, place = lax.axis_index("member"), lax.axis_index("dp")
    core = lax.rem(place, jnp.int32(2))
    chips = gathered.shape[0] // (2 * rows)
    block = feats_ref.shape[0]
    width = columns_ref.shape[1]
    held[slot(mine, block), :] = normed(feats_ref[...], student_gain_ref[...])
    for source, side in ((own_ref, core), (other_ref, 1 - core)):
        for chip in range(chips):
            at = slot(2 * chip + side, rows)
            gathered[at, :] = source[chip * rows : (chip + 1) * rows, :]
        for j in range(members // 2):
            start = chips * rows + j * block
            at = slot(mixed(mine, split_step(j, side, members), members, sender), block)
            held[at, :] = source[start : start + block, :]
    if width % LANES == 0:
        columns_ref[...] = held[:, pl.ds(pl.multiple_of(mine * width, LANES), width)]
    else:
        for j in range(members):

            @pl.when(mine == j)
            def _(j=j):
                columns_ref[...] = held[:, j * width : (j + 1) * width]

    logits = jnp.dot(gathered[...], head_ref[...], preferred_element_type=F32) + bias_ref[...]
    top = jnp.max(logits, axis=1, keepdims=True)
    lse = top + jnp.log(jnp.sum(jnp.exp(logits - top), axis=1, keepdims=True))
    shifted_ref[...] = (logits - lse).astype(BF16)
    lse_ref[...] = jnp.broadcast_to(lse, lse_ref.shape)
    partial_ref[...] = jnp.dot(columns_ref[...], student_ref[...], preferred_element_type=F32)
    classes = logits.shape[1]
    for k in range(members):
        at = slot(mixed(mine, k, members, partner), block)
        out = payloads[k]
        out[0:block, :] = shifted_ref[at, :]
        if k == 0:
            own_logits_ref[...] = partial_ref[at, :] + student_bias_ref[...][None, :]
        out[block : 2 * block, :] = partial_ref[at, :].astype(BF16)
        out[2 * block :, :] = packed3(to_lanes(lse_ref[at, 0:1], classes), PAD, classes)


def alphas_kernel(members, *refs):
    payloads, refs = refs[:1] + refs[1:members][::-1], refs[members:]
    own_logits_ref, alphas_ref, target_ref, small_ref = refs
    mine = lax.axis_index("member")
    block, classes = alphas_ref.shape
    target = jnp.zeros((block, classes), F32)
    logits = own_logits_ref[...]
    lse_total = jnp.zeros((1, LANES), F32)
    small_ref[...] = jnp.zeros_like(small_ref)
    for k in range(members):
        got = payloads[k]
        target += got[0:block, :].astype(F32)
        if k > 0:
            logits += got[block : 2 * block, :].astype(F32)
        tail = got[2 * block :, 0:LANES].astype(F32)
        lse = tail[0:1, :] + tail[1:2, :] + tail[2:3, :]
        lse_total += lse
        small_ref[pl.ds(mixed(mine, k, members, sender), 1), :] = lse
    target = target * (1.0 / members)
    alphas = jnp.exp(logits)
    alphas_ref[...] = alphas
    target_ref[...] = target
    sums = to_lanes(jnp.sum(alphas, axis=1, keepdims=True), LANES)
    parts = to_lanes(
        jnp.sum(log_gamma(alphas, logits) - (alphas - 1.0) * target, axis=1, keepdims=True), LANES
    )
    small_ref[members : members + 1, :] = sums
    small_ref[members + 1 : members + 2, :] = parts - lse_total * (1.0 / members) * (
        sums - float(classes)
    )


def digamma_kernel(alphas_ref, target_ref, columns_ref, inner_ref, turned_ref):
    turned_ref[...] = columns_ref[...].T
    inner_ref[...] = di_gamma(alphas_ref[...]) - target_ref[...]


def joined(parts, members):
    top = functools.reduce(jnp.maximum, parts)
    logs = top + jnp.log(sum(jnp.exp(part - top) for part in parts))
    line = lax.broadcasted_iota(jnp.int32, top.shape, 0)
    return jnp.where(line < members, logs, sum(parts))


def combine_kernel(members, own_ref, other_ref, out_ref):
    out_ref[...] = joined([own_ref[...], other_ref[...]], members)


def signal_kernel(members, chips, images, classes, *refs):
    smalls, refs = refs[:chips], refs[chips:]
    own_ref, alphas_ref, inner_ref, signal_ref, held = refs
    chip = lax.axis_index("dp") // 2
    block = alphas_ref.shape[0]
    for k in range(chips):
        held[mixed(chip, k, chips, sender)] = smalls[k][...]
    everything = joined([held[k] for k in range(chips)], members)
    norm_total = jnp.sum(everything[0:members, :], axis=0, keepdims=True) * (1.0 / members)
    own = jnp.sum(own_ref[0:members, :], axis=0, keepdims=True) * (1.0 / members)
    used = lax.broadcasted_iota(jnp.int32, (1, LANES), 1) < block
    alpha_sum = jnp.where(used, everything[members : members + 1, :], 1.0)
    shift = to_column(di_gamma(alpha_sum) + own - norm_total, block)
    width = alphas_ref.shape[1]
    signal_ref[:, 0:width] = (alphas_ref[...] * (inner_ref[...] - shift)).astype(BF16)
    terms = (
        everything[members + 1 : members + 2, :]
        - log_gamma(alpha_sum, jnp.log(alpha_sum))
        + norm_total * (alpha_sum - float(classes))
    )
    loss = jnp.sum(jnp.where(used, terms, 0.0), axis=1, keepdims=True)
    signal_ref[:, width:] = packed3(loss, block, LANES)


def gradient_kernel(members, images, classes, *refs):
    signals, refs = refs[:members], refs[members:]
    turned_ref, loss_ref, grad_ref, bias_ref, held, losses = refs
    mine = lax.axis_index("member")
    block = images // members
    width = held.shape[1]
    for k in range(members):
        at = mixed(mine, k, members, sender)
        held[slot(at, block), :] = signals[k][:, 0:width]
        tail = signals[k][:, width:].astype(F32)
        losses[pl.ds(at, 1), :] = tail[0:1, :] + tail[1:2, :] + tail[2:3, :]
    signal = held[...]
    grad = jnp.dot(turned_ref[...], signal, preferred_element_type=F32)
    grad_ref[...] = grad * (1.0 / images)
    bias_ref[...] = jnp.sum(signal.astype(F32), axis=0) * (1.0 / images)
    loss_ref[0, 0] = jnp.sum(losses[:, 0:1]) * (1.0 / (images * classes))


def call(kernel, out_shape, scratch=(), out_specs=None, flops=0):
    extra = {}
    if flops:
        extra["cost_estimate"] = pl.CostEstimate(flops=flops, bytes_accessed=0, transcendentals=0)
    if out_specs is not None:
        extra["out_specs"] = out_specs
    return pl.pallas_call(
        kernel,
        out_shape=out_shape,
        scratch_shapes=list(scratch),
        compiler_params=pltpu.CompilerParams(vmem_limit_bytes=48 * 1024 * 1024),
        **extra,
    )


def on_device(
    teacher_feats,
    teacher_gain,
    teacher_head,
    teacher_bias,
    student_feats,
    student_gain,
    student_head,
    student_bias,
):
    members, peers = lax.axis_size("member"), lax.axis_size("dp")
    chips = peers // 2
    shape = jax.ShapeDtypeStruct
    here = pl.BlockSpec(memory_space=pltpu.VMEM)
    feats = teacher_feats[0]
    rows, depth = feats.shape
    block = student_feats.shape[0]
    images = rows * peers
    width, classes = student_head.shape
    small_rows = -(-(members + 2) // 8) * 8

    first = call(first_kernel, shape((8, LANES), F32), flops=1 << 28)()
    students = call(
        student_kernel, shape((members // 2 * block, depth), BF16), flops=1 << 33
    )(*[send_split(student_feats, j) for j in range(members // 2)], student_gain[None], first)
    parts = [feats] + [send(feats, "dp", k, 2) for k in range(1, chips)]
    own = call(
        functools.partial(join_kernel, chips),
        shape((chips * rows + members // 2 * block, depth), BF16),
        flops=1 << 33,
    )(*parts, teacher_gain, students)
    *payloads, own_logits, own_columns = call(
        functools.partial(logits_kernel, members, rows),
        [shape((2 * block + PAD, classes), BF16)] * members
        + [shape((block, classes), F32), shape((images, width), BF16)],
        [
            pltpu.VMEM((images, depth), BF16),
            pltpu.VMEM((images, depth), BF16),
            pltpu.VMEM((images, classes), BF16),
            pltpu.VMEM((images, LANES), F32),
            pltpu.VMEM((images, classes), F32),
        ],
    )(
        own,
        swap_cores(own, "dp"),
        student_feats,
        student_gain[None],
        teacher_head[0],
        student_head,
        teacher_bias,
        student_bias,
    )
    got = [payloads[0]] + [send(payloads[k], "member", k) for k in range(1, members)]
    alphas, target, own = call(
        functools.partial(alphas_kernel, members),
        [shape((block, classes), F32)] * 2 + [shape((small_rows, LANES), F32)],
    )(got[0], *got[1:][::-1], own_logits)
    other = swap_cores(own, "dp")
    inner, turned = call(
        digamma_kernel, [shape((block, classes), F32), shape((width, images), BF16)]
    )(alphas, target, own_columns)
    small = call(functools.partial(combine_kernel, members), shape(own.shape, F32))(own, other)
    smalls = [small] + [send(small, "dp", k, 2) for k in range(1, chips)]
    signal = call(
        functools.partial(signal_kernel, members, chips, images, classes * peers),
        shape((block, classes + LANES), BF16),
        [pltpu.VMEM((chips, small_rows, LANES), F32)],
    )(*smalls, own, alphas, inner)
    signals = [signal] + [send(signal, "member", k) for k in range(1, members)]
    loss, head_grad, bias_grad = call(
        functools.partial(gradient_kernel, members, images, classes * peers),
        [shape((1, 1), F32), shape((width, classes), F32), shape((classes,), F32)],
        [pltpu.VMEM((images, classes), BF16), pltpu.VMEM((members, LANES), F32)],
        out_specs=[pl.BlockSpec(memory_space=pltpu.SMEM), here, here],
    )(*signals, turned)
    return (loss[0, 0], head_grad, bias_grad)


def solution(mesh):
    placed = (
        P("member", "dp", None),
        P("member", None),
        P("member", None, "dp"),
        P("member", "dp"),
        P("member", None),
        P(),
        P("member", "dp"),
        P("dp"),
    )
    return jax.shard_map(
        on_device,
        mesh=mesh,
        in_specs=placed,
        out_specs=(P(), P("member", "dp"), P("dp")),
        check_vma=False,
    )
```

```python
import functools
import math

import jax
import jax.numpy as jnp
from jax import lax
from jax.experimental import pallas as pl
from jax.experimental.pallas import tpu as pltpu
from jax.sharding import PartitionSpec as P

BF16, F32 = jnp.bfloat16, jnp.float32
LANES = 128
PAD = 8
LANCZOS = (
    0.99999999999980993227684700473478,
    676.520368121885098567009190444019,
    -1259.13921672240287047156078755283,
    771.3234287776530788486528258894,
    -176.61502916214059906584551354,
    12.507343278686904814458936853,
    -0.13857109526572011689554707,
    9.984369578019570859563e-6,
    1.50563273514931155834e-7,
)


def partner(index, k, size):
    return index ^ k if size & (size - 1) == 0 else (index + k) % size


def sender(index, k, size):
    return index ^ k if size & (size - 1) == 0 else (index - k + size) % size


def mixed(index, k, size, of):
    if size & (size - 1) == 0:
        return lax.bitwise_xor(index, jnp.int32(k) if isinstance(k, int) else k)
    step = k if of is partner else size - k
    return lax.rem(index + step, jnp.int32(size))


def send(value, axis, k, scale=1, groups=1):
    size = lax.axis_size(axis) // scale
    pairs = [
        (outer * scale + inner, partner(outer, k, size) * scale + inner)
        for outer in range(size)
        for inner in range(scale)
    ]
    return lax.ppermute(value, axis, pairs)


def split_step(j, core, members):
    return jnp.where(core == 1, 2 * j + 1, 2 * j + 2 if 2 * j + 2 < members else 1)


def send_split(value, j):
    members, peers = lax.axis_size("member"), lax.axis_size("dp")
    steps = 2 * j + 1, (2 * j + 2 if 2 * j + 2 < members else 1)
    pairs = [
        (m * peers + d, partner(m, steps[1 - d % 2], members) * peers + d)
        for m in range(members)
        for d in range(peers)
    ]
    return lax.ppermute(value, ("member", "dp"), pairs)


def swap_cores(value, axis):
    return lax.ppermute(value, axis, [(i, i ^ 1) for i in range(lax.axis_size(axis))])


def normed(values, gain_row):
    values = values.astype(F32)
    center = values - jnp.mean(values, axis=-1, keepdims=True)
    spread = jnp.mean(center * center, axis=-1, keepdims=True)
    return (center * lax.rsqrt(spread + 1e-06) * gain_row).astype(BF16)


def split3(value):
    high = value.astype(BF16)
    rest = value - high.astype(F32)
    middle = rest.astype(BF16)
    return high, middle, (rest - middle.astype(F32)).astype(BF16)


def diagonal(rows, lanes):
    return lax.broadcasted_iota(jnp.int32, (rows, lanes), 0) == lax.broadcasted_iota(
        jnp.int32, (rows, lanes), 1
    )


def to_lanes(column, lanes):
    return jnp.sum(
        jnp.where(diagonal(column.shape[0], lanes), column, 0.0), axis=0, keepdims=True
    )


def to_column(row, rows):
    return jnp.sum(jnp.where(diagonal(rows, row.shape[1]), row, 0.0), axis=1, keepdims=True)


def series(x):
    total = jnp.full_like(x, LANCZOS[0])
    slope = jnp.zeros_like(x)
    for k in range(1, 9):
        inverse = 1.0 / (x + float(k))
        term = LANCZOS[k] * inverse
        total = total + term
        slope = slope - term * inverse
    log_t = math.log(7.5) + jnp.log1p(x / 7.5)
    return total, slope, log_t


def log_gamma(x, log_x):
    total, _, log_t = series(x)
    t = x + 7.5
    return (
        (x + 0.5 - t / log_t) * log_t
        + 0.5 * math.log(2.0 * math.pi)
        + jnp.log(total)
        - log_x
    )


def di_gamma(x):
    total, slope, log_t = series(x)
    return log_t + slope / total - 7.0 / (x + 7.5) - 1.0 / x


def slot(at, rows):
    return pl.ds(pl.multiple_of(at * rows, rows), rows)


def first_kernel(out_ref):
    out_ref[...] = jnp.zeros_like(out_ref)


def student_kernel(members, own_ref, *refs):
    *parts, gain_ref, _, own_out, split_out, held, picked = refs
    mine = lax.axis_index("member")
    half, width = own_ref.shape[0] // 2, own_out.shape[1]
    for j, part in enumerate([own_ref] + parts):
        held[...] = normed(part[...], gain_ref[...])
        if width % LANES == 0:
            picked[...] = held[:, pl.ds(pl.multiple_of(mine * width, LANES), width)]
        else:
            for m in range(members):

                @pl.when(mine == m)
                def _(m=m):
                    picked[...] = held[:, m * width : (m + 1) * width]

        if j == 0:
            own_out[...] = picked[...]
            continue
        for h in range(2):
            at = (2 * (j - 1) + h) * width
            split_out[:, at : at + width] = picked[h * half : (h + 1) * half, :]


def join_kernel(chips, *refs):
    *parts, gain_ref, student_ref, out_ref = refs
    chip = lax.axis_index("dp") // 2
    rows = parts[0].shape[0]
    for k in range(chips):
        out_ref[slot(mixed(chip, k, chips, sender), rows), :] = normed(parts[k][...], gain_ref[...])
    start = chips * rows
    out_ref[start:, :] = student_ref[...]


def packed3(row, rows, lanes):
    line = lax.broadcasted_iota(jnp.int32, (rows, lanes), 0)
    high, middle, low = (part.astype(F32) for part in split3(row))
    lower = jnp.where(line == 2, low, 0.0)
    return jnp.where(line == 0, high, jnp.where(line == 1, middle, lower)).astype(BF16)


def logits_kernel(members, rows, *refs):
    own_ref, other_ref, refs = refs[0], refs[1], refs[2:]
    students_ref, head_ref, student_ref, bias_ref, student_bias_ref = refs[:5]
    refs = refs[5:]
    payloads, refs = refs[:members], refs[members:]
    own_logits_ref, columns_ref, gathered, shifted_ref, lse_ref, partial_ref = refs
    mine, place = lax.axis_index("member"), lax.axis_index("dp")
    core = lax.rem(place, jnp.int32(2))
    chips = gathered.shape[0] // (2 * rows)
    block, width = students_ref.shape
    half = block // 2
    columns_ref[slot(mine, block), :] = students_ref[...]
    for source, side in ((own_ref, core), (other_ref, 1 - core)):
        for chip in range(chips):
            at = slot(2 * chip + side, rows)
            gathered[at, :] = source[chip * rows : (chip + 1) * rows, :]
        for j in range(members // 2):
            at = mixed(mine, split_step(j, side, members), members, sender)
            for h in range(2):
                piece = (2 * j + h) * width
                columns_ref[slot(2 * at + h, half), :] = source[chips * rows :, piece : piece + width]
    logits = jnp.dot(gathered[...], head_ref[...], preferred_element_type=F32) + bias_ref[...]
    top = jnp.max(logits, axis=1, keepdims=True)
    lse = top + jnp.log(jnp.sum(jnp.exp(logits - top), axis=1, keepdims=True))
    shifted_ref[...] = (logits - lse).astype(BF16)
    lse_ref[...] = jnp.broadcast_to(lse, lse_ref.shape)
    partial_ref[...] = jnp.dot(columns_ref[...], student_ref[...], preferred_element_type=F32)
    classes = logits.shape[1]
    for k in range(members):
        at = slot(mixed(mine, k, members, partner), block)
        out = payloads[k]
        out[0:block, :] = shifted_ref[at, :]
        if k == 0:
            own_logits_ref[...] = partial_ref[at, :] + student_bias_ref[...][None, :]
        out[block : 2 * block, :] = partial_ref[at, :].astype(BF16)
        out[2 * block :, :] = packed3(to_lanes(lse_ref[at, 0:1], classes), PAD, classes)


def alphas_kernel(members, *refs):
    payloads, refs = refs[:1] + refs[1:members][::-1], refs[members:]
    own_logits_ref, alphas_ref, target_ref, small_ref = refs
    mine = lax.axis_index("member")
    block, classes = alphas_ref.shape
    target = jnp.zeros((block, classes), F32)
    logits = own_logits_ref[...]
    lse_total = jnp.zeros((1, LANES), F32)
    small_ref[...] = jnp.zeros_like(small_ref)
    for k in range(members):
        got = payloads[k]
        target += got[0:block, :].astype(F32)
        if k > 0:
            logits += got[block : 2 * block, :].astype(F32)
        tail = got[2 * block :, 0:LANES].astype(F32)
        lse = tail[0:1, :] + tail[1:2, :] + tail[2:3, :]
        lse_total += lse
        small_ref[pl.ds(mixed(mine, k, members, sender), 1), :] = lse
    target = target * (1.0 / members)
    alphas = jnp.exp(logits)
    alphas_ref[...] = alphas
    target_ref[...] = target
    sums = to_lanes(jnp.sum(alphas, axis=1, keepdims=True), LANES)
    parts = to_lanes(
        jnp.sum(log_gamma(alphas, logits) - (alphas - 1.0) * target, axis=1, keepdims=True), LANES
    )
    small_ref[members : members + 1, :] = sums
    small_ref[members + 1 : members + 2, :] = parts - lse_total * (1.0 / members) * (
        sums - float(classes)
    )


def digamma_kernel(alphas_ref, target_ref, columns_ref, inner_ref, turned_ref):
    turned_ref[...] = columns_ref[...].T
    inner_ref[...] = di_gamma(alphas_ref[...]) - target_ref[...]


def joined(parts, members):
    top = functools.reduce(jnp.maximum, parts)
    logs = top + jnp.log(sum(jnp.exp(part - top) for part in parts))
    line = lax.broadcasted_iota(jnp.int32, top.shape, 0)
    return jnp.where(line < members, logs, sum(parts))


def combine_kernel(members, own_ref, other_ref, out_ref):
    out_ref[...] = joined([own_ref[...], other_ref[...]], members)


def signal_kernel(members, chips, images, classes, *refs):
    smalls, refs = refs[:chips], refs[chips:]
    own_ref, alphas_ref, inner_ref, signal_ref, held = refs
    chip = lax.axis_index("dp") // 2
    block = alphas_ref.shape[0]
    for k in range(chips):
        held[mixed(chip, k, chips, sender)] = smalls[k][...]
    everything = joined([held[k] for k in range(chips)], members)
    norm_total = jnp.sum(everything[0:members, :], axis=0, keepdims=True) * (1.0 / members)
    own = jnp.sum(own_ref[0:members, :], axis=0, keepdims=True) * (1.0 / members)
    used = lax.broadcasted_iota(jnp.int32, (1, LANES), 1) < block
    alpha_sum = jnp.where(used, everything[members : members + 1, :], 1.0)
    shift = to_column(di_gamma(alpha_sum) + own - norm_total, block)
    width = alphas_ref.shape[1]
    signal_ref[0:block, :] = (alphas_ref[...] * (inner_ref[...] - shift)).astype(BF16)
    terms = (
        everything[members + 1 : members + 2, :]
        - log_gamma(alpha_sum, jnp.log(alpha_sum))
        + norm_total * (alpha_sum - float(classes))
    )
    loss = jnp.sum(jnp.where(used, terms, 0.0), axis=1, keepdims=True)
    signal_ref[block:, :] = packed3(loss, PAD, width)


def gradient_kernel(members, images, classes, *refs):
    signals, refs = refs[:members], refs[members:]
    turned_ref, loss_ref, grad_ref, bias_ref, held, losses = refs
    mine = lax.axis_index("member")
    block = images // members
    for k in range(members):
        at = mixed(mine, k, members, sender)
        held[slot(at, block), :] = signals[k][0:block, :]
        tail = signals[k][block:, 0:LANES].astype(F32)
        losses[pl.ds(at, 1), :] = tail[0:1, :] + tail[1:2, :] + tail[2:3, :]
    signal = held[...]
    grad = jnp.dot(turned_ref[...], signal, preferred_element_type=F32)
    grad_ref[...] = grad * (1.0 / images)
    bias_ref[...] = jnp.sum(signal.astype(F32), axis=0) * (1.0 / images)
    loss_ref[0, 0] = jnp.sum(losses[:, 0:1]) * (1.0 / (images * classes))


def call(kernel, out_shape, scratch=(), out_specs=None, flops=0):
    extra = {}
    if flops:
        extra["cost_estimate"] = pl.CostEstimate(flops=flops, bytes_accessed=0, transcendentals=0)
    if out_specs is not None:
        extra["out_specs"] = out_specs
    return pl.pallas_call(
        kernel,
        out_shape=out_shape,
        scratch_shapes=list(scratch),
        compiler_params=pltpu.CompilerParams(vmem_limit_bytes=48 * 1024 * 1024),
        **extra,
    )


def on_device(
    teacher_feats,
    teacher_gain,
    teacher_head,
    teacher_bias,
    student_feats,
    student_gain,
    student_head,
    student_bias,
):
    members, peers = lax.axis_size("member"), lax.axis_size("dp")
    chips = peers // 2
    shape = jax.ShapeDtypeStruct
    here = pl.BlockSpec(memory_space=pltpu.VMEM)
    feats = teacher_feats[0]
    rows, depth = feats.shape
    block = student_feats.shape[0]
    images = rows * peers
    width, classes = student_head.shape
    small_rows = -(-(members + 2) // 8) * 8

    first = call(first_kernel, shape((8, LANES), F32), flops=1 << 28)()
    own_students, students = call(
        functools.partial(student_kernel, members),
        [shape((block, width), BF16), shape((block // 2, depth), BF16)],
        [pltpu.VMEM((block, depth), BF16), pltpu.VMEM((block, width), BF16)],
        flops=1 << 33,
    )(
        student_feats,
        *[send_split(student_feats, j) for j in range(members // 2)],
        student_gain[None],
        first,
    )
    parts = [feats] + [send(feats, "dp", k, 2) for k in range(1, chips)]
    own = call(
        functools.partial(join_kernel, chips),
        shape((chips * rows + block // 2, depth), BF16),
        flops=1 << 33,
    )(*parts, teacher_gain, students)
    *payloads, own_logits, own_columns = call(
        functools.partial(logits_kernel, members, rows),
        [shape((2 * block + PAD, classes), BF16)] * members
        + [shape((block, classes), F32), shape((images, width), BF16)],
        [
            pltpu.VMEM((images, depth), BF16),
            pltpu.VMEM((images, classes), BF16),
            pltpu.VMEM((images, LANES), F32),
            pltpu.VMEM((images, classes), F32),
        ],
    )(
        own,
        swap_cores(own, "dp"),
        own_students,
        teacher_head[0],
        student_head,
        teacher_bias,
        student_bias,
    )
    got = [payloads[0]] + [send(payloads[k], "member", k) for k in range(1, members)]
    alphas, target, own = call(
        functools.partial(alphas_kernel, members),
        [shape((block, classes), F32)] * 2 + [shape((small_rows, LANES), F32)],
    )(got[0], *got[1:][::-1], own_logits)
    other = swap_cores(own, "dp")
    inner, turned = call(
        digamma_kernel, [shape((block, classes), F32), shape((width, images), BF16)]
    )(alphas, target, own_columns)
    small = call(functools.partial(combine_kernel, members), shape(own.shape, F32))(own, other)
    smalls = [small] + [send(small, "dp", k, 2) for k in range(1, chips)]
    signal = call(
        functools.partial(signal_kernel, members, chips, images, classes * peers),
        shape((block + PAD, classes), BF16),
        [pltpu.VMEM((chips, small_rows, LANES), F32)],
    )(*smalls, own, alphas, inner)
    signals = [signal] + [send(signal, "member", k) for k in range(1, members)]
    loss, head_grad, bias_grad = call(
        functools.partial(gradient_kernel, members, images, classes * peers),
        [shape((1, 1), F32), shape((width, classes), F32), shape((classes,), F32)],
        [pltpu.VMEM((images, classes), BF16), pltpu.VMEM((members, LANES), F32)],
        out_specs=[pl.BlockSpec(memory_space=pltpu.SMEM), here, here],
    )(*signals, turned)
    return (loss[0, 0], head_grad, bias_grad)


def solution(mesh):
    placed = (
        P("member", "dp", None),
        P("member", None),
        P("member", None, "dp"),
        P("member", "dp"),
        P("member", None),
        P(),
        P("member", "dp"),
        P("dp"),
    )
    return jax.shard_map(
        on_device,
        mesh=mesh,
        in_specs=placed,
        out_specs=(P(), P("member", "dp"), P("dp")),
        check_vma=False,
    )
```

```python
import functools
import math

import jax
import jax.numpy as jnp
from jax import lax
from jax.experimental import pallas as pl
from jax.experimental.pallas import tpu as pltpu
from jax.sharding import PartitionSpec as P

BF16, F32 = jnp.bfloat16, jnp.float32
LANES = 128
PAD = 8
LANCZOS = (
    0.99999999999980993227684700473478,
    676.520368121885098567009190444019,
    -1259.13921672240287047156078755283,
    771.3234287776530788486528258894,
    -176.61502916214059906584551354,
    12.507343278686904814458936853,
    -0.13857109526572011689554707,
    9.984369578019570859563e-6,
    1.50563273514931155834e-7,
)


def partner(index, k, size):
    return index ^ k if size & (size - 1) == 0 else (index + k) % size


def sender(index, k, size):
    return index ^ k if size & (size - 1) == 0 else (index - k + size) % size


def mixed(index, k, size, of):
    if size & (size - 1) == 0:
        return lax.bitwise_xor(index, jnp.int32(k) if isinstance(k, int) else k)
    step = k if of is partner else size - k
    return lax.rem(index + step, jnp.int32(size))


def send(value, axis, k, scale=1, groups=1):
    size = lax.axis_size(axis) // scale
    pairs = [
        (outer * scale + inner, partner(outer, k, size) * scale + inner)
        for outer in range(size)
        for inner in range(scale)
    ]
    return lax.ppermute(value, axis, pairs)


def split_steps(j, members):
    return max(members - 2 - 2 * j, 1), members - 1 - 2 * j


def split_step(j, core, members):
    steps = split_steps(j, members)
    return jnp.where(core == 0, steps[0], steps[1])


def send_split(value, j):
    members, peers = lax.axis_size("member"), lax.axis_size("dp")
    steps = split_steps(j, members)
    pairs = [
        (m * peers + d, partner(m, steps[d % 2], members) * peers + d)
        for m in range(members)
        for d in range(peers)
    ]
    return lax.ppermute(value, ("member", "dp"), pairs)


def swap_cores(value, axis):
    return lax.ppermute(value, axis, [(i, i ^ 1) for i in range(lax.axis_size(axis))])


def normed(values, gain_row):
    values = values.astype(F32)
    center = values - jnp.mean(values, axis=-1, keepdims=True)
    spread = jnp.mean(center * center, axis=-1, keepdims=True)
    return (center * lax.rsqrt(spread + 1e-06) * gain_row).astype(BF16)


def split3(value):
    high = value.astype(BF16)
    rest = value - high.astype(F32)
    middle = rest.astype(BF16)
    return high, middle, (rest - middle.astype(F32)).astype(BF16)


def diagonal(rows, lanes):
    return lax.broadcasted_iota(jnp.int32, (rows, lanes), 0) == lax.broadcasted_iota(
        jnp.int32, (rows, lanes), 1
    )


def to_lanes(column, lanes):
    return jnp.sum(
        jnp.where(diagonal(column.shape[0], lanes), column, 0.0), axis=0, keepdims=True
    )


def to_column(row, rows):
    return jnp.sum(jnp.where(diagonal(rows, row.shape[1]), row, 0.0), axis=1, keepdims=True)


def series(x):
    total = jnp.full_like(x, LANCZOS[0])
    slope = jnp.zeros_like(x)
    for k in range(1, 9):
        inverse = 1.0 / (x + float(k))
        term = LANCZOS[k] * inverse
        total = total + term
        slope = slope - term * inverse
    log_t = math.log(7.5) + jnp.log1p(x / 7.5)
    return total, slope, log_t


def log_gamma(x, log_x):
    total, _, log_t = series(x)
    t = x + 7.5
    return (
        (x + 0.5 - t / log_t) * log_t
        + 0.5 * math.log(2.0 * math.pi)
        + jnp.log(total)
        - log_x
    )


def di_gamma(x):
    total, slope, log_t = series(x)
    return log_t + slope / total - 7.0 / (x + 7.5) - 1.0 / x


def slot(at, rows):
    return pl.ds(pl.multiple_of(at * rows, rows), rows)


def first_kernel(out_ref):
    out_ref[...] = jnp.zeros_like(out_ref)


def student_kernel(members, own_ref, *refs):
    *parts, gain_ref, _, own_out, split_out, held, picked = refs
    mine = lax.axis_index("member")
    half, width = own_ref.shape[0] // 2, own_out.shape[1]
    for j, part in enumerate([own_ref] + parts):
        held[...] = normed(part[...], gain_ref[...])
        if width % LANES == 0:
            picked[...] = held[:, pl.ds(pl.multiple_of(mine * width, LANES), width)]
        else:
            for m in range(members):

                @pl.when(mine == m)
                def _(m=m):
                    picked[...] = held[:, m * width : (m + 1) * width]

        if j == 0:
            own_out[...] = picked[...]
            continue
        for h in range(2):
            at = (2 * (j - 1) + h) * width
            split_out[:, at : at + width] = picked[h * half : (h + 1) * half, :]


def join_kernel(chips, *refs):
    *parts, gain_ref, student_ref, out_ref = refs
    chip = lax.axis_index("dp") // 2
    rows = parts[0].shape[0]
    for k in range(chips):
        out_ref[slot(mixed(chip, k, chips, sender), rows), :] = normed(parts[k][...], gain_ref[...])
    start = chips * rows
    out_ref[start:, :] = student_ref[...]


def packed3(row, rows, lanes):
    line = lax.broadcasted_iota(jnp.int32, (rows, lanes), 0)
    high, middle, low = (part.astype(F32) for part in split3(row))
    lower = jnp.where(line == 2, low, 0.0)
    return jnp.where(line == 0, high, jnp.where(line == 1, middle, lower)).astype(BF16)


def logits_kernel(members, rows, *refs):
    own_ref, other_ref, refs = refs[0], refs[1], refs[2:]
    students_ref, head_ref, student_ref, bias_ref, student_bias_ref = refs[:5]
    refs = refs[5:]
    payloads, refs = refs[:members], refs[members:]
    own_logits_ref, columns_ref, gathered, shifted_ref, lse_ref, partial_ref = refs
    mine, place = lax.axis_index("member"), lax.axis_index("dp")
    core = lax.rem(place, jnp.int32(2))
    chips = gathered.shape[0] // (2 * rows)
    block, width = students_ref.shape
    half = block // 2
    columns_ref[slot(mine, block), :] = students_ref[...]
    for source, side in ((own_ref, core), (other_ref, 1 - core)):
        for chip in range(chips):
            at = slot(2 * chip + side, rows)
            gathered[at, :] = source[chip * rows : (chip + 1) * rows, :]
        for j in range(members // 2):
            at = mixed(mine, split_step(j, side, members), members, sender)
            for h in range(2):
                piece = (2 * j + h) * width
                columns_ref[slot(2 * at + h, half), :] = source[chips * rows :, piece : piece + width]
    logits = jnp.dot(gathered[...], head_ref[...], preferred_element_type=F32) + bias_ref[...]
    top = jnp.max(logits, axis=1, keepdims=True)
    lse = top + jnp.log(jnp.sum(jnp.exp(logits - top), axis=1, keepdims=True))
    shifted_ref[...] = (logits - lse).astype(BF16)
    lse_ref[...] = jnp.broadcast_to(lse, lse_ref.shape)
    partial_ref[...] = jnp.dot(columns_ref[...], student_ref[...], preferred_element_type=F32)
    classes = logits.shape[1]
    for k in range(members):
        at = slot(mixed(mine, k, members, partner), block)
        out = payloads[k]
        out[0:block, :] = shifted_ref[at, :]
        if k == 0:
            own_logits_ref[...] = partial_ref[at, :] + student_bias_ref[...][None, :]
        out[block : 2 * block, :] = partial_ref[at, :].astype(BF16)
        out[2 * block :, :] = packed3(to_lanes(lse_ref[at, 0:1], classes), PAD, classes)


def alphas_kernel(members, *refs):
    payloads, refs = refs[:1] + refs[1:members][::-1], refs[members:]
    own_logits_ref, alphas_ref, target_ref, small_ref = refs
    mine = lax.axis_index("member")
    block, classes = alphas_ref.shape
    target = jnp.zeros((block, classes), F32)
    logits = own_logits_ref[...]
    lse_total = jnp.zeros((1, LANES), F32)
    small_ref[...] = jnp.zeros_like(small_ref)
    for k in range(members):
        got = payloads[k]
        target += got[0:block, :].astype(F32)
        if k > 0:
            logits += got[block : 2 * block, :].astype(F32)
        tail = got[2 * block :, 0:LANES].astype(F32)
        lse = tail[0:1, :] + tail[1:2, :] + tail[2:3, :]
        lse_total += lse
        small_ref[pl.ds(mixed(mine, k, members, sender), 1), :] = lse
    target = target * (1.0 / members)
    alphas = jnp.exp(logits)
    alphas_ref[...] = alphas
    target_ref[...] = target
    sums = to_lanes(jnp.sum(alphas, axis=1, keepdims=True), LANES)
    parts = to_lanes(
        jnp.sum(log_gamma(alphas, logits) - (alphas - 1.0) * target, axis=1, keepdims=True), LANES
    )
    small_ref[members : members + 1, :] = sums
    small_ref[members + 1 : members + 2, :] = parts - lse_total * (1.0 / members) * (
        sums - float(classes)
    )


def digamma_kernel(alphas_ref, target_ref, columns_ref, inner_ref, turned_ref):
    turned_ref[...] = columns_ref[...].T
    inner_ref[...] = di_gamma(alphas_ref[...]) - target_ref[...]


def joined(parts, members):
    top = functools.reduce(jnp.maximum, parts)
    logs = top + jnp.log(sum(jnp.exp(part - top) for part in parts))
    line = lax.broadcasted_iota(jnp.int32, top.shape, 0)
    return jnp.where(line < members, logs, sum(parts))


def combine_kernel(members, own_ref, other_ref, out_ref):
    out_ref[...] = joined([own_ref[...], other_ref[...]], members)


def signal_kernel(members, chips, images, classes, *refs):
    smalls, refs = refs[:chips], refs[chips:]
    own_ref, alphas_ref, inner_ref, signal_ref, held = refs
    chip = lax.axis_index("dp") // 2
    block = alphas_ref.shape[0]
    for k in range(chips):
        held[mixed(chip, k, chips, sender)] = smalls[k][...]
    everything = joined([held[k] for k in range(chips)], members)
    norm_total = jnp.sum(everything[0:members, :], axis=0, keepdims=True) * (1.0 / members)
    own = jnp.sum(own_ref[0:members, :], axis=0, keepdims=True) * (1.0 / members)
    used = lax.broadcasted_iota(jnp.int32, (1, LANES), 1) < block
    alpha_sum = jnp.where(used, everything[members : members + 1, :], 1.0)
    shift = to_column(di_gamma(alpha_sum) + own - norm_total, block)
    width = alphas_ref.shape[1]
    signal_ref[0:block, :] = (alphas_ref[...] * (inner_ref[...] - shift)).astype(BF16)
    terms = (
        everything[members + 1 : members + 2, :]
        - log_gamma(alpha_sum, jnp.log(alpha_sum))
        + norm_total * (alpha_sum - float(classes))
    )
    loss = jnp.sum(jnp.where(used, terms, 0.0), axis=1, keepdims=True)
    signal_ref[block:, :] = packed3(loss, PAD, width)


def gradient_kernel(members, images, classes, *refs):
    signals, refs = refs[:members], refs[members:]
    turned_ref, loss_ref, grad_ref, bias_ref, held, losses = refs
    mine = lax.axis_index("member")
    block = images // members
    for k in range(members):
        at = mixed(mine, k, members, sender)
        held[slot(at, block), :] = signals[k][0:block, :]
        tail = signals[k][block:, 0:LANES].astype(F32)
        losses[pl.ds(at, 1), :] = tail[0:1, :] + tail[1:2, :] + tail[2:3, :]
    signal = held[...]
    grad = jnp.dot(turned_ref[...], signal, preferred_element_type=F32)
    grad_ref[...] = grad * (1.0 / images)
    bias_ref[...] = jnp.sum(signal.astype(F32), axis=0) * (1.0 / images)
    loss_ref[0, 0] = jnp.sum(losses[:, 0:1]) * (1.0 / (images * classes))


def call(kernel, out_shape, scratch=(), out_specs=None, flops=0):
    extra = {}
    if flops:
        extra["cost_estimate"] = pl.CostEstimate(flops=flops, bytes_accessed=0, transcendentals=0)
    if out_specs is not None:
        extra["out_specs"] = out_specs
    return pl.pallas_call(
        kernel,
        out_shape=out_shape,
        scratch_shapes=list(scratch),
        compiler_params=pltpu.CompilerParams(vmem_limit_bytes=48 * 1024 * 1024),
        **extra,
    )


def on_device(
    teacher_feats,
    teacher_gain,
    teacher_head,
    teacher_bias,
    student_feats,
    student_gain,
    student_head,
    student_bias,
):
    members, peers = lax.axis_size("member"), lax.axis_size("dp")
    chips = peers // 2
    shape = jax.ShapeDtypeStruct
    here = pl.BlockSpec(memory_space=pltpu.VMEM)
    feats = teacher_feats[0]
    rows, depth = feats.shape
    block = student_feats.shape[0]
    images = rows * peers
    width, classes = student_head.shape
    small_rows = -(-(members + 2) // 8) * 8

    first = call(first_kernel, shape((8, LANES), F32), flops=1 << 28)()
    own_students, students = call(
        functools.partial(student_kernel, members),
        [shape((block, width), BF16), shape((block // 2, depth), BF16)],
        [pltpu.VMEM((block, depth), BF16), pltpu.VMEM((block, width), BF16)],
        flops=1 << 33,
    )(
        student_feats,
        *[send_split(student_feats, j) for j in range(members // 2)],
        student_gain[None],
        first,
    )
    parts = [feats] + [send(feats, "dp", k, 2) for k in range(1, chips)]
    own = call(
        functools.partial(join_kernel, chips),
        shape((chips * rows + block // 2, depth), BF16),
        flops=1 << 33,
    )(*parts, teacher_gain, students)
    *payloads, own_logits, own_columns = call(
        functools.partial(logits_kernel, members, rows),
        [shape((2 * block + PAD, classes), BF16)] * members
        + [shape((block, classes), F32), shape((images, width), BF16)],
        [
            pltpu.VMEM((images, depth), BF16),
            pltpu.VMEM((images, classes), BF16),
            pltpu.VMEM((images, LANES), F32),
            pltpu.VMEM((images, classes), F32),
        ],
    )(
        own,
        swap_cores(own, "dp"),
        own_students,
        teacher_head[0],
        student_head,
        teacher_bias,
        student_bias,
    )
    got = [payloads[0]] + [send(payloads[k], "member", k) for k in range(1, members)]
    alphas, target, own = call(
        functools.partial(alphas_kernel, members),
        [shape((block, classes), F32)] * 2 + [shape((small_rows, LANES), F32)],
    )(got[0], *got[1:][::-1], own_logits)
    other = swap_cores(own, "dp")
    inner, turned = call(
        digamma_kernel, [shape((block, classes), F32), shape((width, images), BF16)]
    )(alphas, target, own_columns)
    small = call(functools.partial(combine_kernel, members), shape(own.shape, F32))(own, other)
    smalls = [small] + [send(small, "dp", k, 2) for k in range(1, chips)]
    signal = call(
        functools.partial(signal_kernel, members, chips, images, classes * peers),
        shape((block + PAD, classes), BF16),
        [pltpu.VMEM((chips, small_rows, LANES), F32)],
    )(*smalls, own, alphas, inner)
    signals = [signal] + [send(signal, "member", k) for k in range(1, members)]
    loss, head_grad, bias_grad = call(
        functools.partial(gradient_kernel, members, images, classes * peers),
        [shape((1, 1), F32), shape((width, classes), F32), shape((classes,), F32)],
        [pltpu.VMEM((images, classes), BF16), pltpu.VMEM((members, LANES), F32)],
        out_specs=[pl.BlockSpec(memory_space=pltpu.SMEM), here, here],
    )(*signals, turned)
    return (loss[0, 0], head_grad, bias_grad)


def solution(mesh):
    placed = (
        P("member", "dp", None),
        P("member", None),
        P("member", None, "dp"),
        P("member", "dp"),
        P("member", None),
        P(),
        P("member", "dp"),
        P("dp"),
    )
    return jax.shard_map(
        on_device,
        mesh=mesh,
        in_specs=placed,
        out_specs=(P(), P("member", "dp"), P("dp")),
        check_vma=False,
    )
```
